256 devices in a mesh: depth: 32 (over z, y), heads: 8 (over x, core).
Axes of the slice: x: 4, y: 4, z: 8, core: 2. Of those that a mesh axis runs over, the one named last changes fastest.
Arguments:
- q_raw: bfloat16 [8192, 8192], P('depth', 'heads'), may hold values from -60 to 60
- k_raw: bfloat16 [8192, 1024], P('depth', 'heads'), may hold values from -60 to 60
- values: bfloat16 [8192, 1024], P('depth', 'heads'), may hold values from -6 to 6
- q_gain: float32 [128], replicated, may hold values from 0.7 to 6
- k_gain: float32 [128], replicated, may hold values from 0.7 to 6
- grad_out: bfloat16 [8192, 8192], P('depth', 'heads'), may hold values from -6 to 6
- block_mask: int32 [64, 64], replicated, may hold values from 0 to 1, as said below
- block_count: int32 [64], replicated, may hold values from 64 to 128, as said below
Outputs:
- out: bfloat16 [8192, 8192], P('depth', 'heads')
- grad_q: bfloat16 [8192, 8192], P('depth', 'heads')
- grad_k: bfloat16 [8192, 1024], P('depth', 'heads')
- grad_values: bfloat16 [8192, 1024], P('depth', 'heads')
- grad_q_gain: float32 [128], replicated
- grad_k_gain: float32 [128], replicated
The draws below stay inside these ranges and needn't reach their ends.
Inputs may be any that keep to these rules, and one draw needn't show every extreme that they name: Blocks 2 * j to 2 * j + 1 form level j of a forest of 32 levels whose two roots are blocks 0 and 1; each block of level j > 0 has one parent in level j - 1; block_mask[b, c] = 1 exactly when c is b or an ancestor of b, so row b holds exactly one 1 in each level up to b's own and none deeper. `block_count`: block 0 is full.
All inputs are finite; a program needn't handle non-finite values.
Results may differ from the reference program's by a relative error of at most 0.035.
The reference program's roundings to bfloat16 on the way (of `q_low`, `k_low`, `prob_low` and `grad_score`) count: a program that leaves them out, or rounds other values in their place, can miss the bound.
Values may be sent and summed in bfloat16 or wider, within the bound.
A program may use at most 128 MiB of HBM per device.

```python
import jax
import jax.numpy as jnp
from jax import lax

DH = 128
QHEADS = 64
KVHEADS = 8
BLOCK = 128
BLK_DEV = 2
LEVELS = 32
NBLK = 64
TOKENS = 8192


def draw_q_raw(key, part):
    key = jax.random.fold_in(key, 1)
    noise_rows = jnp.clip(jax.random.normal(key, (NBLK, BLOCK, QHEADS, DH), jnp.float32), -6.0, 6.0)
    return noise_rows.reshape(TOKENS, QHEADS * DH).astype(jnp.bfloat16)


def draw_k_raw(key, part):
    key = jax.random.fold_in(key, 2)
    noise_rows = jnp.clip(jax.random.normal(key, (NBLK, BLOCK, KVHEADS, DH), jnp.float32), -6.0, 6.0)
    return noise_rows.reshape(TOKENS, KVHEADS * DH).astype(jnp.bfloat16)


def draw_q_gain(key, part):
    key = jax.random.fold_in(key, 3)
    return jax.random.uniform(key, (DH,), jnp.float32, 0.7, 1.3)


def draw_k_gain(key, part):
    key = jax.random.fold_in(key, 4)
    return jax.random.uniform(key, (DH,), jnp.float32, 0.7, 1.3)


def draw_block_mask(key, part):
    key = jax.random.fold_in(key, 8)
    pick_parent = jax.random.randint(key, (NBLK,), 0, BLK_DEV).astype(jnp.int32)
    block_ids = jnp.arange(NBLK, dtype=jnp.int32)
    level_of = block_ids // BLK_DEV
    parent = jnp.where(level_of > 0, (level_of - 1) * BLK_DEV + pick_parent, block_ids).astype(jnp.int32)
    identity = (block_ids[:, None] == block_ids[None, :]).astype(jnp.int32)

    def extend(step_number, closure):
        return jnp.maximum(identity, closure[parent])
    return lax.fori_loop(0, LEVELS, extend, identity)


def draw_block_count(key, part):
    key = jax.random.fold_in(key, 9)
    counts_drawn = jax.random.randint(key, (NBLK,), BLOCK // 2, BLOCK + 1).astype(jnp.int32)
    return counts_drawn.at[0].set(BLOCK)


def block_scale(own_key, shape, cuts, smallest, top_value):
    level = 1.0
    for axis_at, blocks in cuts:
        draws = jax.random.uniform(jax.random.fold_in(jax.random.fold_in(own_key, 6), axis_at), (blocks,), jnp.float32, smallest / len(cuts), top_value / len(cuts))
        level = level * jnp.repeat(jnp.exp(draws), shape[axis_at] // blocks).reshape((-1,) + (1,) * (len(shape) - 1 - axis_at))
    return level


def normal_values(rng, shape, deviation, limit, cuts=(), held_as=jnp.bfloat16):
    array = deviation * jax.random.normal(rng, shape, jnp.float32)
    if cuts:
        array = array * block_scale(rng, shape, cuts, -0.22, 0.18)
    return jnp.clip(array, -limit, limit).astype(held_as)


def setup_inputs(seed: int = 0) -> dict:
    seeds = jax.random.split(jax.random.key(seed), 9)
    return {
        "q_raw": draw_q_raw(jax.random.fold_in(seeds[8], 71), 0),
        "k_raw": draw_k_raw(jax.random.fold_in(seeds[8], 71), 0),
        "values": normal_values(seeds[2], (TOKENS, KVHEADS * DH), 1.0, 6.0, ((0, 32), (1, 8))),
        "q_gain": draw_q_gain(jax.random.fold_in(seeds[8], 71), 0),
        "k_gain": draw_k_gain(jax.random.fold_in(seeds[8], 71), 0),
        "grad_out": normal_values(seeds[5], (TOKENS, QHEADS * DH), 1.0, 6.0, ((0, 32), (1, 8))),
        "block_mask": draw_block_mask(jax.random.fold_in(seeds[8], 71), 0),
        "block_count": draw_block_count(jax.random.fold_in(seeds[8], 71), 0),
    }


EPSILON = 1e-06

def normalize(raw_rows, gain):
    values_f = raw_rows.astype(jnp.float32)
    inverse = 1.0 / jnp.sqrt(lax.optimization_barrier(jnp.mean(values_f * values_f, axis=-1, keepdims=True)) + EPSILON)
    normed = values_f * inverse
    return (normed, inverse, (normed * gain).astype(jnp.bfloat16))

def norm_backward(grad_in, normed, inverse, gain):
    grad_hat = grad_in * gain
    inner_mean = lax.optimization_barrier(jnp.mean(grad_hat * normed, axis=-1, keepdims=True))
    grad_raw = inverse * (grad_hat - normed * inner_mean)
    gain_part = lax.optimization_barrier(jnp.sum((grad_in * normed).reshape(-1, normed.shape[-1]), axis=0))
    return (grad_raw, gain_part)

def reference(q_raw, k_raw, values, q_gain, k_gain, grad_out, block_mask, block_count):
    group_size = QHEADS // KVHEADS
    scale_factor = DH ** (-0.5)
    k_hat, k_inv, k_low = normalize(k_raw.reshape(TOKENS, KVHEADS, DH), k_gain)
    keys_all = k_low.reshape(NBLK, BLOCK, KVHEADS, DH)
    values_all = values.reshape(NBLK, BLOCK, KVHEADS, DH)
    q_blocks = q_raw.reshape(NBLK, BLOCK, KVHEADS, group_size, DH)
    g_blocks = grad_out.reshape(NBLK, BLOCK, KVHEADS, group_size, DH)
    places = jnp.arange(BLOCK, dtype=jnp.int32)
    level_ids = jnp.arange(LEVELS, dtype=jnp.int32)
    member_ids = jnp.arange(BLK_DEV, dtype=jnp.int32)

    def one_block(loop_carry, inputs):
        partial_value, gain_acc = loop_carry
        query_rows, grad_rows, block_id = inputs
        q_hat, q_inv, q_low = normalize(query_rows, q_gain)
        level_rows = block_mask[block_id].reshape(LEVELS, BLK_DEV)
        ancestors = (level_ids * BLK_DEV + lax.optimization_barrier(jnp.sum(level_rows * member_ids[None, :], axis=1))).astype(jnp.int32)
        alive_levels = lax.optimization_barrier(jnp.sum(level_rows, axis=1))
        tile_keys = keys_all[ancestors].reshape(LEVELS * BLOCK, KVHEADS, DH).astype(jnp.float32)
        tile_values = values_all[ancestors].reshape(LEVELS * BLOCK, KVHEADS, DH).astype(jnp.float32)
        key_counts = block_count[ancestors]
        allowed = (alive_levels[:, None] > 0) & (places[None, :] < key_counts[:, None])
        allowed = allowed[None, :, :] & ((ancestors[None, :, None] != block_id) | (places[None, None, :] <= places[:, None, None]))
        allowed = allowed.reshape(BLOCK, LEVELS * BLOCK)
        scores = jnp.einsum('qgjd,kgd->gjqk', q_low.astype(jnp.float32), tile_keys) * scale_factor
        scores = jnp.where(allowed[None, None], scores, -jnp.inf)
        row_top = lax.optimization_barrier(jnp.max(scores, axis=-1, keepdims=True))
        weights = jnp.exp(scores - row_top)
        prob_full = weights / lax.optimization_barrier(jnp.sum(weights, axis=-1, keepdims=True))
        prob_low = prob_full.astype(jnp.bfloat16)
        out_rows = jnp.einsum('gjqk,kgd->qgjd', prob_low.astype(jnp.float32), tile_values).astype(jnp.bfloat16)
        grad_f = grad_rows.astype(jnp.float32)
        row_delta = jnp.einsum('qgjd,qgjd->gjq', grad_f, out_rows.astype(jnp.float32))
        grad_prob = jnp.einsum('qgjd,kgd->gjqk', grad_f, tile_values)
        grad_score = (prob_full * (grad_prob - row_delta[..., None])).astype(jnp.bfloat16).astype(jnp.float32)
        grad_qn = jnp.einsum('gjqk,kgd->qgjd', grad_score, tile_keys) * scale_factor
        grad_kn = jnp.einsum('gjqk,qgjd->kgd', grad_score, q_low.astype(jnp.float32)) * scale_factor
        grad_vn = jnp.einsum('gjqk,qgjd->kgd', prob_low.astype(jnp.float32), grad_f)
        pieces = jnp.stack([grad_kn, grad_vn], axis=2).reshape(LEVELS, BLOCK, KVHEADS, 2, DH)
        partial_value = partial_value.at[ancestors].add(pieces)
        grad_rows_q, gain_part = norm_backward(grad_qn, q_hat, q_inv, q_gain)
        return ((partial_value, gain_acc + gain_part), (out_rows, grad_rows_q.astype(jnp.bfloat16)))
    start_partial = jnp.zeros((NBLK, BLOCK, KVHEADS, 2, DH), jnp.float32)
    start_gain = jnp.zeros((DH,), jnp.float32)
    block_ids = jnp.arange(NBLK, dtype=jnp.int32)
    (partial_value, q_gain_grad), (out_rows, grad_q_rows) = lax.scan(one_block, (start_partial, start_gain), (q_blocks, g_blocks, block_ids))
    grad_kn_all = partial_value[:, :, :, 0, :].reshape(TOKENS, KVHEADS, DH)
    grad_k, k_gain_grad = norm_backward(grad_kn_all, k_hat, k_inv, k_gain)
    grad_values = partial_value[:, :, :, 1, :].reshape(TOKENS, KVHEADS * DH).astype(jnp.bfloat16)
    return (out_rows.reshape(TOKENS, QHEADS * DH), grad_q_rows.reshape(TOKENS, QHEADS * DH), grad_k.astype(jnp.bfloat16).reshape(TOKENS, KVHEADS * DH), grad_values, q_gain_grad, k_gain_grad)
```

```python
import functools
import heapq
import math

import jax
import jax.numpy as jnp
from jax import lax
from jax.experimental import pallas as pl
from jax.experimental.pallas import tpu as pltpu
from jax.sharding import PartitionSpec as P

DH = 128
BLOCK = 128
EPS = 1e-6
SCALE = DH ** -0.5
C2 = SCALE * math.log2(math.e)
NEG = -1e30
f32 = jnp.float32
bf16 = jnp.bfloat16
MESH = pl.DeviceIdType.MESH

def dot(a,b): return jnp.dot(a,b,preferred_element_type=f32)
def dott(a,b): return lax.dot_general(a,b,(((0,),(0,)),((),())),preferred_element_type=f32)

def attn_kernel(pos_fn, LC, RT, LEVELS, AUG, mask_ref, count_ref, q_ref, g_ref, qg_ref, ka_ref, va_ref,
                out_ref, gq_ref, pk_ref, pv_ref, qgp_ref,
                kx, vx, s_scr, qT, gT, qrows, grows, ot, dqt, dk, dv, ml):
    pos = pos_fn()
    nl = pos + 1
    nch = (nl + LC - 1) // LC
    CK = LC*BLOCK
    R = 8*BLOCK
    NRT = R//RT
    KA = 256 if AUG else 128
    gain = qg_ref[...]
    lane = lax.broadcasted_iota(jnp.int32, (BLOCK, BLOCK), 1)
    sub = lax.broadcasted_iota(jnp.int32, (BLOCK, BLOCK), 0)
    causal = jnp.where(sub <= lane, 0.0, NEG).astype(f32)
    if RT > BLOCK:
        causal = jnp.concatenate([causal]*(RT//BLOCK), axis=1)

    def block(b, gacc):
        rows = pl.ds(pl.multiple_of(b*BLOCK, BLOCK), BLOCK)
        own = 2*pos + b
        def gather(s, _):
            lev = jnp.maximum(s-1, 0)
            lev = jnp.minimum(lev, LEVELS-1)
            pick = jnp.where(s == 0, own, 2*lev + mask_ref[own, 2*lev+1])
            live = s < nl
            cnt = jnp.where(live, count_ref[pick], 0)
            ks = pl.ds(pl.multiple_of(s*BLOCK, BLOCK), BLOCK)
            kx[ks, 0:128] = ka_ref[pick]
            vx[ks, 0:128] = va_ref[pick]
            bias = jnp.where(sub < cnt, 0.0, NEG)
            kx[ks, 128:256] = jnp.where(lane == 0, bias, 0.0).astype(bf16)
            vx[ks, 128:256] = jnp.where(lane < 3, -1.0, 0.0).astype(bf16)
            return 0
        lax.fori_loop(0, nch*LC, gather, 0)
        qT[128:256, :] = jnp.where(lax.broadcasted_iota(jnp.int32, (128, R), 0) == 0, 1.0, 0.0).astype(bf16)
        for h in range(8):
            hs = slice(h*128, (h+1)*128)
            qf = q_ref[rows, hs].astype(f32)
            inv = 1.0/jnp.sqrt(jnp.mean(qf*qf, axis=-1, keepdims=True) + EPS)
            low = (qf*inv*gain).astype(bf16)
            qrows[hs, :] = low
            qT[0:128, hs] = low.T
            gr = g_ref[rows, hs]
            grows[hs, :] = gr
            gT[0:128, hs] = gr.T
        ml[0:1, :] = jnp.full((1, R), NEG, f32)
        ml[1:2, :] = jnp.zeros((1, R), f32)

        def pass1(c, first):
            ks = pl.ds(pl.multiple_of(c*CK, CK), CK)
            kc = kx[ks, :]
            for r in range(NRT):
                rs = slice(r*RT, (r+1)*RT)
                s = dot(kc, qT[:, rs])
                if first:
                    s = jnp.concatenate([s[0:BLOCK] + causal, s[BLOCK:]], axis=0) if LC > 1 else s + causal
                s_scr[ks, rs] = s
                mo = ml[0:1, rs]
                mn = jnp.maximum(mo, jnp.max(s, axis=0, keepdims=True))
                e = jnp.exp2((s - mn)*C2)
                ml[1:2, rs] = ml[1:2, rs]*jnp.exp2((mo-mn)*C2) + jnp.sum(e, axis=0, keepdims=True)
                ml[0:1, rs] = mn
        pass1(0, True)
        def p1(c, _):
            pass1(c, False)
            return 0
        lax.fori_loop(1, nch, p1, 0)
        ml[2:3, :] = ml[0:1, :]*C2 + jnp.log2(ml[1:2, :])
        ot[...] = jnp.zeros_like(ot)
        dqt[...] = jnp.zeros_like(dqt)

        def p3(c, _):
            ks = pl.ds(pl.multiple_of(c*CK, CK), CK)
            vc = vx[ks, 0:128]
            acc = None
            for r in range(NRT):
                rs = slice(r*RT, (r+1)*RT)
                p = jnp.exp2(s_scr[ks, rs]*C2 - ml[2:3, rs])
                s_scr[ks, rs] = p
                lo = p.astype(bf16)
                ot[:, rs] += dott(vc, lo)
                t = dot(lo, grows[rs, :])
                acc = t if acc is None else acc + t
            dv[b, ks, :] = acc
            return 0
        lax.fori_loop(0, nch, p3, 0)
        olow = ot[...].astype(bf16)
        delta = jnp.sum(olow.astype(f32)*gT[0:128, :].astype(f32), axis=0, keepdims=True)
        d0 = delta.astype(bf16); r1 = delta - d0.astype(f32)
        d1 = r1.astype(bf16); d2 = (r1 - d1.astype(f32)).astype(bf16)
        z = lax.broadcasted_iota(jnp.int32, (128, R), 0)
        gT[128:256, :] = jnp.where(z == 0, d0.astype(f32), jnp.where(z == 1, d1.astype(f32), jnp.where(z == 2, d2.astype(f32), 0.0))).astype(bf16)
        for h in range(8):
            hs = slice(h*128, (h+1)*128)
            out_ref[rows, hs] = olow[:, hs].T

        def p4(c, _):
            ks = pl.ds(pl.multiple_of(c*CK, CK), CK)
            vc = vx[ks, :]
            kc = kx[ks, 0:128]
            acc = None
            for r in range(NRT):
                rs = slice(r*RT, (r+1)*RT)
                dp = dot(vc, gT[:, rs])
                ds = (s_scr[ks, rs]*dp).astype(bf16)
                dqt[:, rs] += dott(kc, ds)
                t = dot(ds, qrows[rs, :])
                acc = t if acc is None else acc + t
            dk[b, ks, :] = acc*SCALE
            return 0
        lax.fori_loop(0, nch, p4, 0)
        for h in range(8):
            hs = slice(h*128, (h+1)*128)
            gqn = dqt[:, hs].T*SCALE
            qf = q_ref[rows, hs].astype(f32)
            inv = 1.0/jnp.sqrt(jnp.mean(qf*qf, axis=-1, keepdims=True) + EPS)
            hat = qf*inv
            gh = gqn*gain
            im = jnp.mean(gh*hat, axis=-1, keepdims=True)
            gq_ref[rows, hs] = (inv*(gh - hat*im)).astype(bf16)
            gacc = gacc + jnp.sum(gqn*hat, axis=0, keepdims=True)
        return gacc
    qgp_ref[...] = lax.fori_loop(0, 2, block, jnp.zeros((1, 128), f32))

    def combine(i, _):
        ks = pl.ds(pl.multiple_of((i+1)*BLOCK, BLOCK), BLOCK)
        p0 = mask_ref[2*pos, 2*i+1]
        p1_ = mask_ref[2*pos+1, 2*i+1]
        for (src, dst) in ((dk, pk_ref), (dv, pv_ref)):
            a0 = src[0, ks, :]; a1 = src[1, ks, :]
            for m in range(2):
                x = jnp.where(p0 == m, a0, 0.0) + jnp.where(p1_ == m, a1, 0.0)
                dst[i, m*BLOCK:(m+1)*BLOCK, :] = x.astype(bf16)
        return 0
    lax.fori_loop(0, pos, combine, 0)
    for (src, dst) in ((dk, pk_ref), (dv, pv_ref)):
        for b in range(2):
            dst[pos, b*BLOCK:(b+1)*BLOCK, :] = src[b, 0:BLOCK, :].astype(bf16)
    def zero(i, _):
        pk_ref[i] = jnp.zeros((2*BLOCK, DH), bf16)
        pv_ref[i] = jnp.zeros((2*BLOCK, DH), bf16)
        return 0
    lax.fori_loop(pos+1, LEVELS, zero, 0)

def attention(pos_fn, mask, count, q, g, qg, ka, va, LC=16, RT=256, LEVELS=32, AUG=True):
    V=pl.BlockSpec(memory_space=pltpu.VMEM); S=pl.BlockSpec(memory_space=pltpu.SMEM)
    KT=LEVELS*BLOCK
    R=1024
    sd=jax.ShapeDtypeStruct
    return pl.pallas_call(
        functools.partial(attn_kernel, pos_fn, LC, RT, LEVELS, AUG),
        out_shape=(sd((256,1024),bf16), sd((256,1024),bf16), sd((LEVELS,256,128),bf16), sd((LEVELS,256,128),bf16), sd((1,128),f32)),
        in_specs=[S,S,V,V,V,V,V], out_specs=(V,)*5,
        scratch_shapes=[pltpu.VMEM((KT,256),bf16), pltpu.VMEM((KT,256),bf16), pltpu.VMEM((KT,R),f32),
            pltpu.VMEM((256,R),bf16), pltpu.VMEM((256,R),bf16), pltpu.VMEM((R,128),bf16), pltpu.VMEM((R,128),bf16),
            pltpu.VMEM((128,R),f32), pltpu.VMEM((128,R),f32), pltpu.VMEM((2,KT,128),f32), pltpu.VMEM((2,KT,128),f32), pltpu.VMEM((8,R),f32)],
        compiler_params=pltpu.CompilerParams(vmem_limit_bytes=60*2**20),
        name="attention",
    )(mask, count, q, g, qg, ka, va)

NZ, NY = 8, 4
STEP={"z+":(1,0),"z-":(-1,0),"y+":(0,1),"y-":(0,-1)}

def build_trees():
    parent={}
    for buf in range(2):
        for oz in range(NZ):
            for oy in range(NY):
                if (oz,oy)==(0,0): continue
                zdir="z+" if oz>4 else "z-"
                ydir={3:"y+",1:"y-"}.get(oy)
                if buf==0:
                    if oz==0: d=ydir or "y+"
                    elif oy==2 and oz%2==1: d="y+" if oz in (1,5) else "y-"
                    else:
                        d=zdir if oz!=4 else ("z+" if oy in (0,2) else "z-")
                else:
                    if oy==0: d=zdir if oz!=4 else "z+"
                    else: d=ydir or ("y+" if oz%2==0 else "y-")
                parent[buf,oz,oy]=d
    children={}
    for (buf,oz,oy),d in parent.items():
        sz,sy=STEP[d]
        src=(buf,(oz+sz)%NZ,(oy+sy)%NY)
        children.setdefault(src,[]).append((d,(buf,oz,oy)))
    return parent,children

def plan():
    parent,children=build_trees()
    def depth(x):
        return 1+max([depth(c) for _,c in children.get(x,[])],default=0)
    heaps={d:[] for d in STEP}
    n=0
    def push(x):
        nonlocal n
        for d,c in children.get(x,[]):
            heapq.heappush(heaps[d],(-depth(c),n,c)); n+=1
    for buf in range(2): push((buf,0,0))
    order=[]; rounds=0
    while any(heaps.values()):
        got=[]
        for d in STEP:
            if heaps[d]: got.append(heapq.heappop(heaps[d])[2])
        got.sort(key=lambda x:-depth(x))
        for c in got: order.append(c); push(c)
        rounds+=1
    return parent,children,order,rounds

PARENT,CHILDREN,ORDER,ROUNDS=plan()
INDEX={x:i for i,x in enumerate(ORDER)}

def coords():
    p=lax.axis_index("depth")
    return p//NY, p%NY
def level(z,y,oz,oy):
    return lax.rem(z+oz+NZ,NZ)*NY+lax.rem(y+oy+NY,NY)
def toward(z,y,d):
    return {"depth": level(z,y,*STEP[d])}

def ag_kernel(k_ref,v_ref,kg_ref,ka,va,klow,send_sem,recv_sem,lsem):
    z,y=coords()
    me=z*NY+y
    bar=pltpu.get_barrier_semaphore()
    for d in STEP:
        pl.semaphore_signal(bar,inc=1,device_id=toward(z,y,d),device_id_type=MESH)
    kf=k_ref[...].astype(f32)
    inv=1.0/jnp.sqrt(jnp.mean(kf*kf,axis=-1,keepdims=True)+EPS)
    klow[...]=(kf*inv*kg_ref[...]).astype(bf16)
    pl.semaphore_wait(bar,4)
    outs=(ka,va); own=(klow,v_ref)
    started=[]
    def send(x):
        buf,oz,oy=x
        lev=level(z,y,oz,oy)
        for d,c in CHILDREN.get(x,[]):
            i=INDEX[c]
            src=own[buf] if (oz,oy)==(0,0) else outs[buf].at[lev]
            cp=pltpu.make_async_remote_copy(src_ref=src,dst_ref=outs[buf].at[lev],send_sem=send_sem.at[i],recv_sem=recv_sem.at[i],device_id=toward(z,y,d),device_id_type=MESH)
            cp.start(); started.append(cp)
    for buf in range(2): send((buf,0,0))
    locs=[]
    for buf in range(2):
        cp=pltpu.make_async_copy(own[buf],outs[buf].at[me],lsem.at[buf]); cp.start(); locs.append(cp)
    for x in ORDER:
        buf,oz,oy=x
        lev=level(z,y,oz,oy); i=INDEX[x]
        pltpu.make_async_remote_copy(src_ref=own[buf],dst_ref=outs[buf].at[lev],send_sem=send_sem.at[i],recv_sem=recv_sem.at[i],device_id=toward(z,y,"z+"),device_id_type=MESH).wait_recv()
        send(x)
    for cp in started: cp.wait_send()
    for cp in locs: cp.wait()

def all_gather(k,v,kg,space=pl.ANY):
    rows=k.shape[0]
    sd=jax.ShapeDtypeStruct
    V=pl.BlockSpec(memory_space=pltpu.VMEM); A=pl.BlockSpec(memory_space=space)
    n=len(ORDER)
    return pl.pallas_call(ag_kernel,out_shape=(sd((NZ*NY,rows,128),bf16),)*2,in_specs=[V,V,V],out_specs=(A,A),
        scratch_shapes=[pltpu.VMEM((rows,128),bf16),pltpu.SemaphoreType.DMA((n,)),pltpu.SemaphoreType.DMA((n,)),pltpu.SemaphoreType.DMA((2,))],
        compiler_params=pltpu.CompilerParams(collective_id=0,has_side_effects=True),name="gather_kv")(k,v,kg)

def rs_kernel(nh,pk,pv,k_ref,kg_ref,qgp_ref,gk_ref,gv_ref,qg_out,kg_out,land,stage,arh,arz,ary,send_sem,recv_sem,ars,arr):
    z,y=coords(); h=lax.axis_index("heads")
    me=z*NY+y
    bar=pltpu.get_barrier_semaphore()
    peers=[({"heads":lax.rem(h+j,nh)}) for j in range(1,nh)]
    zp=[{"depth":level(z,y,j,0)} for j in range(1,NZ)]
    yp=[{"depth":level(z,y,0,j)} for j in range(1,NY)]
    allp=peers+zp+yp
    for d in allp:
        pl.semaphore_signal(bar,inc=1,device_id=d,device_id_type=MESH)
    pl.semaphore_wait(bar,len(allp))
    parts=(pk,pv)
    started=[]
    def recv(c):
        i=INDEX[c]
        pltpu.make_async_remote_copy(src_ref=land.at[i],dst_ref=land.at[i],send_sem=send_sem.at[i],recv_sem=recv_sem.at[i],device_id=toward(z,y,"z+"),device_id_type=MESH).wait_recv()
    back={"z+":"z-","z-":"z+","y+":"y-","y-":"y+"}
    def total(x):
        buf,oz,oy=x
        s=parts[buf][level(z,y,oz,oy)].astype(f32)
        for _,c in CHILDREN.get(x,[]):
            recv(c)
            s=s+land[INDEX[c]].astype(f32)
        return s
    for x in reversed(ORDER):
        buf,oz,oy=x; i=INDEX[x]
        lev=level(z,y,oz,oy)
        if CHILDREN.get(x):
            stage[i]=total(x).astype(bf16)
            src=stage.at[i]
        else:
            src=parts[buf].at[lev]
        cp=pltpu.make_async_remote_copy(src_ref=src,dst_ref=land.at[i],send_sem=send_sem.at[i],recv_sem=recv_sem.at[i],device_id=toward(z,y,back[PARENT[x]]),device_id_type=MESH)
        cp.start(); started.append(cp)
    gkn=total((0,0,0))
    kf=k_ref[...].astype(f32)
    inv=1.0/jnp.sqrt(jnp.mean(kf*kf,axis=-1,keepdims=True)+EPS)
    hat=kf*inv
    part=jnp.concatenate([qgp_ref[...],jnp.sum(gkn*hat,axis=0,keepdims=True),jnp.zeros((6,128),f32)],axis=0)
    def stage_ar(buf,mine,n,base,mkid,part):
        cps=[]
        buf[mine]=part
        for j in range(1,n):
            cp=pltpu.make_async_remote_copy(src_ref=buf.at[mine],dst_ref=buf.at[mine],send_sem=ars.at[base+j-1],recv_sem=arr.at[base+j-1],device_id=mkid(j),device_id_type=MESH)
            cp.start(); cps.append(cp)
        return cps
    def finish_ar(buf,n,cps):
        for cp in cps: cp.wait_recv()
        s=buf[0]
        for j in range(1,n): s=s+buf[j]
        return s
    c1=stage_ar(arh,h,nh,0,lambda j:{"heads":lax.rem(h+j,nh)},part)
    gh=gkn*kg_ref[...]
    im=jnp.mean(gh*hat,axis=-1,keepdims=True)
    gk_ref[...]=(inv*(gh-hat*im)).astype(bf16)
    gv_ref[...]=total((1,0,0)).astype(bf16)
    t=finish_ar(arh,nh,c1)
    c2=stage_ar(arz,z,NZ,nh-1,lambda j:{"depth":level(z,y,j,0)},t)
    t=finish_ar(arz,NZ,c2)
    c3=stage_ar(ary,y,NY,nh-1+NZ-1,lambda j:{"depth":level(z,y,0,j)},t)
    t=finish_ar(ary,NY,c3)
    qg_out[...]=t[0:1]; kg_out[...]=t[1:2]
    for cp in started+c1+c2+c3: cp.wait_send()

def reduce_scatter(pk,pv,k,kg,qgp,nh):
    rows=k.shape[0]
    sd=jax.ShapeDtypeStruct
    V=pl.BlockSpec(memory_space=pltpu.VMEM)
    n=len(ORDER); na=nh-1+NZ-1+NY-1
    return pl.pallas_call(functools.partial(rs_kernel,nh),
        out_shape=(sd((rows,128),bf16),sd((rows,128),bf16),sd((1,128),f32),sd((1,128),f32)),
        in_specs=[V]*5,out_specs=(V,)*4,
        scratch_shapes=[pltpu.VMEM((n,rows,128),bf16),pltpu.VMEM((n,rows,128),bf16),pltpu.VMEM((nh,8,128),f32),pltpu.VMEM((NZ,8,128),f32),pltpu.VMEM((NY,8,128),f32),
            pltpu.SemaphoreType.DMA((n,)),pltpu.SemaphoreType.DMA((n,)),pltpu.SemaphoreType.DMA((na,)),pltpu.SemaphoreType.DMA((na,))],
        compiler_params=pltpu.CompilerParams(collective_id=1,has_side_effects=True,vmem_limit_bytes=56*2**20),name="scatter_kv")(pk,pv,k,kg,qgp)


def body(q_raw, k_raw, values, q_gain, k_gain, grad_out, block_mask, block_count):
    kg = k_gain.reshape(1, DH)
    qg = q_gain.reshape(1, DH)
    ka, va = all_gather(k_raw, values, kg)
    ka = ka.reshape(2 * NZ * NY, BLOCK, DH)
    va = va.reshape(2 * NZ * NY, BLOCK, DH)
    out, gq, pk, pv, qgp = attention(
        lambda: lax.axis_index("depth"), block_mask, block_count, q_raw, grad_out, qg, ka, va
    )
    gk, gv, qgg, kgg = reduce_scatter(pk, pv, k_raw, kg, qgp, lax.axis_size("heads"))
    return out, gq, gk, gv, qgg.reshape(DH), kgg.reshape(DH)


def solution(mesh):
    rows = P("depth", "heads")
    return jax.shard_map(
        body,
        mesh=mesh,
        in_specs=(rows, rows, rows, P(), P(), rows, P(), P()),
        out_specs=(rows, rows, rows, rows, P(), P()),
        check_vma=False,
    )
```

```python
import functools
import math

import jax
import jax.numpy as jnp
from jax import lax
from jax.experimental import pallas as pl
from jax.experimental.pallas import tpu as pltpu
from jax.sharding import PartitionSpec as P

f32 = jnp.float32
bf16 = jnp.bfloat16
MESH = pl.DeviceIdType.MESH
DH = 128
BLOCK = 128
EPS = 1e-6
SCALE = DH ** -0.5
C2 = SCALE * math.log2(math.e)
NEG = -1e30
NZ, NY = 8, 4
HALVES = 2
LATENCY = 2.0*HALVES

STEP = {"z+": (1, 0), "z-": (-1, 0), "y+": (0, 1), "y-": (0, -1)}
BACK = {"z+": "z-", "z-": "z+", "y+": "y-", "y-": "y+"}
PARTS = [(t, s) for t in range(2) for s in range(HALVES)]


def build_trees():
    parent = {}
    for part in PARTS:
        z_last = (part[1] if HALVES == 2 else part[0]) == 0
        for oz in range(NZ):
            for oy in range(NY):
                if (oz, oy) == (0, 0):
                    continue
                zdir = "z+" if oz > NZ // 2 else "z-"
                ydir = {3: "y+", 1: "y-"}.get(oy)
                if z_last:
                    if oz == 0:
                        d = ydir or "y+"
                    elif oy == 2 and oz % 2 == 1:
                        d = "y+" if oz in (1, 5) else "y-"
                    elif oz == NZ // 2:
                        d = "z+" if oy in (0, 2) else "z-"
                    else:
                        d = zdir
                elif oy == 0:
                    d = "z+" if oz == NZ // 2 else zdir
                else:
                    d = ydir or ("y+" if oz % 2 == 0 else "y-")
                parent[part, oz, oy] = d
    children = {}
    for (part, oz, oy), d in parent.items():
        sz, sy = STEP[d]
        children.setdefault((part, (oz + sz) % NZ, (oy + sy) % NY), []).append((d, (part, oz, oy)))
    return parent, children


PARENT, CHILDREN = build_trees()


def height(x):
    return 1 + max([height(c) for _, c in CHILDREN.get(x, [])], default=0)


def hops(x):
    part, oz, oy = x
    if (oz, oy) == (0, 0):
        return 0
    sz, sy = STEP[PARENT[x]]
    return 1 + hops((part, (oz + sz) % NZ, (oy + sy) % NY))


def needed_planes(x):
    part, oz, oy = x
    offsets = {0}
    stack = [(x, 0)]
    while stack:
        node, dz = stack.pop()
        offsets.add(dz)
        for d, c in CHILDREN.get(node, []):
            stack.append((c, dz + STEP[d][0]))
    return frozenset(z for z in range(NZ) if any((z + dz) % NZ >= (z + oz) % NZ for dz in offsets))


def gather_order():
    waiting, order, count, now = [], [], 0, 0
    free = dict.fromkeys(STEP, 0.0)
    def push(x, at):
        nonlocal count
        for d, c in CHILDREN.get(x, []):
            waiting.append((at, (x[0][0], -height(c), count), d, c))
            count += 1
    for part in PARTS:
        push((part, 0, 0), 0.0)
    done = []
    while waiting:
        start, key, d, c = min((max(free[w[2]], w[0]), w[1], w[2], w[3]) for w in waiting)
        waiting = [w for w in waiting if w[3] != c]
        free[d] = start + 1
        done.append((start + 1 + LATENCY, key, c))
        push(c, start + 1 + LATENCY)
    done.sort()
    return [(c, t) for t, _, c in done]


def scatter_order(first):
    pieces = list(PARENT)
    free = dict.fromkeys(STEP, 0.0)
    arrived, order = {}, []
    left = set(pieces)
    while left:
        best = None
        for x in left:
            kids = CHILDREN.get(x, [])
            if any(c not in arrived for _, c in kids):
                continue
            ready = max([arrived[c] for _, c in kids], default=0.0 if x[0][0] == first else 1.0)
            d = BACK[PARENT[x]]
            key = (max(free[d], ready), x[0][0] != first, -hops(x), PARTS.index(x[0]), x[1], x[2])
            if best is None or key < best[0]:
                best = (key, x, d)
        key, x, d = best
        left.remove(x)
        free[d] = key[0] + 1
        arrived[x] = key[0] + 1 + LATENCY
        order.append((x, key[0]))
    ends = {}
    for part in PARTS:
        ends[part] = max(arrived[c] for _, c in CHILDREN[part, 0, 0])
    return order, ends


GATHER = [x for x, _ in gather_order()]
SCATTER = [x for x, _ in scatter_order(1)[0]]
INDEX = {x: i for i, x in enumerate(GATHER)}
PLANES = {x: needed_planes(x) for x in GATHER}
NPIECE = len(GATHER)


def level(z, y, oz, oy):
    return lax.rem(z + oz + NZ, NZ) * NY + lax.rem(y + oy + NY, NY)


def toward(z, y, d):
    return {"depth": level(z, y, *STEP[d])}


def among(z, planes):
    if len(planes) == NZ:
        return None
    return functools.reduce(jnp.logical_or, [z == p for p in sorted(planes)]) if planes else False


def guarded(cond, fn):
    if cond is None:
        fn()
    elif cond is not False:
        pl.when(cond)(fn)


def shifted(planes, d):
    return frozenset((p - STEP[d][0]) % NZ for p in planes)


def half(ref, lev, part):
    rows = ref.shape[1] // HALVES
    return ref.at[lev, pl.ds(part[1] * rows, rows)]


def copy_to(src, dst, send_sem, recv_sem, i, dev):
    return pltpu.make_async_remote_copy(src_ref=src, dst_ref=dst, send_sem=send_sem.at[i], recv_sem=recv_sem.at[i], device_id=dev, device_id_type=MESH)


def gather_piece(z, y, x, bufs, sems):
    part, oz, oy = x
    ref = half(bufs[part[0]], level(z, y, oz, oy), part)
    return copy_to(ref, ref, *sems, INDEX[x], toward(z, y, "z+"))


def gather_sends(z, y, x, bufs, sems, go):
    part, oz, oy = x
    for d, c in CHILDREN.get(x, []):
        ref = half(bufs[part[0]], level(z, y, oz, oy), part)
        cp = copy_to(ref, ref, *sems, INDEX[c], toward(z, y, d))
        guarded(among(z, shifted(PLANES[c], d)), cp.start if go else cp.wait_send)


def gather_own(z, y, bufs, sems):
    for part in PARTS:
        gather_sends(z, y, (part, 0, 0), bufs, sems, True)


def gather_rest(z, y, bufs, sems):
    for x in GATHER:
        def step(x=x):
            gather_piece(z, y, x, bufs, sems).wait_recv()
            gather_sends(z, y, x, bufs, sems, True)
        guarded(among(z, PLANES[x]), step)


def gather_drain(z, y, bufs, sems):
    for part in PARTS:
        gather_sends(z, y, (part, 0, 0), bufs, sems, False)
    for x in GATHER:
        gather_sends(z, y, x, bufs, sems, False)


def leaf_planes(x):
    out = set(PLANES[x])
    for d, c in CHILDREN.get(x, []):
        out -= shifted(PLANES[c], d)
    return frozenset(out)


def scatter_send(z, y, x, bufs, land, sems):
    part, oz, oy = x
    return copy_to(half(bufs[part[0]], level(z, y, oz, oy), part), land.at[INDEX[x]], *sems, INDEX[x], toward(z, y, BACK[PARENT[x]]))


def scatter_leaves(z, y, tensor, bufs, land, sems):
    for x in SCATTER:
        if x[0][0] == tensor:
            guarded(among(z, leaf_planes(x)), lambda x=x: scatter_send(z, y, x, bufs, land, sems).start())


def scatter_total(z, y, x, bufs, land, sems):
    part, oz, oy = x
    total = half(bufs[part[0]], level(z, y, oz, oy), part)
    kids = [c for d, c in CHILDREN.get(x, [])]
    for d, c in CHILDREN.get(x, []):
        i = INDEX[c]
        arrival = copy_to(land.at[i], land.at[i], *sems, i, toward(z, y, "z+"))
        guarded(among(z, shifted(PLANES[c], d)), arrival.wait_recv)
    total = total[...].astype(f32)
    for c in kids:
        total = total + land[INDEX[c]].astype(f32)
    return total


def scatter_inner(z, y, x, bufs, land, sems):
    part, oz, oy = x
    def step():
        half(bufs[part[0]], level(z, y, oz, oy), part)[...] = scatter_total(z, y, x, bufs, land, sems).astype(bf16)
        scatter_send(z, y, x, bufs, land, sems).start()
    guarded(among(z, PLANES[x] - leaf_planes(x)), step)


def scatter_own(z, y, tensor, bufs, land, sems):
    return jnp.concatenate([scatter_total(z, y, (part, 0, 0), bufs, land, sems) for part in PARTS if part[0] == tensor], axis=0)


def scatter_drain(z, y, bufs, land, sems):
    for x in SCATTER:
        guarded(among(z, PLANES[x]), lambda x=x: scatter_send(z, y, x, bufs, land, sems).wait_send())


def spread(buf, mine, sems, base, n, device, part):
    buf[mine] = part
    copies = []
    for j in range(1, n):
        cp = copy_to(buf.at[mine], buf.at[mine], *sems, base + j - 1, device(j))
        cp.start()
        copies.append(cp)
    return copies


def collect(buf, n, copies):
    for cp in copies:
        cp.wait_recv()
    total = buf[0]
    for j in range(1, n):
        total = total + buf[j]
    return total


def greet(z, y, h, nh):
    peers = [{"heads": lax.rem(h + j, nh)} for j in range(1, nh)]
    peers += [{"depth": level(z, y, j, 0)} for j in range(1, NZ)]
    peers += [{"depth": level(z, y, 0, j)} for j in range(1, NY)]
    bar = pltpu.get_barrier_semaphore()
    for d in peers:
        pl.semaphore_signal(bar, inc=1, device_id=d, device_id_type=MESH)
    return lambda: pl.semaphore_wait(bar, len(peers))

LEVELS = NZ * NY
HEADS = 8
R = HEADS * BLOCK
KT = LEVELS * BLOCK


def dot(a, b):
    return jnp.dot(a, b, preferred_element_type=f32)


def dot_lhs_t(a, b):
    return lax.dot_general(a, b, (((0,), (0,)), ((), ())), preferred_element_type=f32)


def normed(rows):
    x = rows.astype(f32)
    inv = 1.0 / jnp.sqrt(jnp.mean(x * x, axis=-1, keepdims=True) + EPS)
    return x * inv, inv


def norm_backward(grad, hat, inv, gain):
    gh = grad * gain
    return inv * (gh - hat * jnp.mean(gh * hat, axis=-1, keepdims=True))


def fused_kernel(nh, LC, RT, mask_ref, count_ref, q_ref, g_ref, k_ref, v_ref, qg_ref, kg_ref,
                 out_ref, gq_ref, gk_ref, gv_ref, gain_ref,
                 ka, va, kx, vx, s_scr, qT, gT, qrows, grows, ot, dqt, dk, dv, ml, pk, pv, land, o_scr, gq_scr,
                 arh, arz, ary, gsend, grecv, ssend, srecv, asend, arecv, lsem):
    pos = lax.axis_index("depth")
    h = lax.axis_index("heads")
    z, y = pos // NY, pos % NY
    gsem, ssem, asem = (gsend, grecv), (ssend, srecv), (asend, arecv)
    kv, parts = (ka, va), (pk, pv)
    greeted = greet(z, y, h, nh)
    k_hat, k_inv = normed(k_ref[...])
    ka[pos] = (k_hat * kg_ref[...]).astype(bf16)
    va[pos] = v_ref[...]
    land[...] = jnp.zeros_like(land)
    greeted()
    gather_own(z, y, kv, gsem)

    nl = pos + 1
    nch = (nl + LC - 1) // LC
    CK = LC * BLOCK
    NRT = R // RT
    gain = qg_ref[...]
    lane = lax.broadcasted_iota(jnp.int32, (BLOCK, BLOCK), 1)
    sub = lax.broadcasted_iota(jnp.int32, (BLOCK, BLOCK), 0)
    causal = jnp.where(sub <= lane, 0.0, NEG).astype(f32)
    causal = jnp.concatenate([causal] * (RT // BLOCK), axis=1)
    extra = lax.broadcasted_iota(jnp.int32, (BLOCK, R), 0)

    def prepare(b):
        rows = pl.ds(b * BLOCK, BLOCK)
        qT[b, 128:256, :] = jnp.where(extra == 0, 1.0, 0.0).astype(bf16)
        for i in range(HEADS):
            hs = slice(i * 128, (i + 1) * 128)
            hat, inv = normed(q_ref[rows, hs])
            low = (hat * gain).astype(bf16)
            qrows[b, hs, :] = low
            qT[b, 0:128, hs] = low.T
            gr = g_ref[rows, hs]
            grows[b, hs, :] = gr
            gT[b, 0:128, hs] = gr.T

    for b in range(2):
        prepare(b)

    def fill(i, _):
        pk[i] = jnp.zeros((2 * BLOCK, DH), bf16)
        pv[i] = jnp.zeros((2 * BLOCK, DH), bf16)
        return 0

    lax.fori_loop(nl, LEVELS, fill, 0)
    gather_rest(z, y, kv, gsem)

    def chunk(c):
        return pl.ds(pl.multiple_of(c * CK, CK), CK)

    def combine(src, dst):
        def one(i, _):
            ks = pl.ds(pl.multiple_of((i + 1) * BLOCK, BLOCK), BLOCK)
            m0 = mask_ref[2 * pos, 2 * i + 1]
            m1 = mask_ref[2 * pos + 1, 2 * i + 1]
            a0 = src[0, ks, :]
            a1 = src[1, ks, :]
            for m in range(2):
                both = jnp.where(m0 == m, a0, 0.0) + jnp.where(m1 == m, a1, 0.0)
                dst[i, m * BLOCK:(m + 1) * BLOCK, :] = both.astype(bf16)
            return 0

        lax.fori_loop(0, pos, one, 0)
        for b in range(2):
            dst[pos, b * BLOCK:(b + 1) * BLOCK, :] = src[b, 0:BLOCK, :].astype(bf16)

    q_part = jnp.zeros((1, DH), f32)
    ml[3:4, 0:DH] = jnp.zeros((1, DH), f32)
    for b in range(2):
        own = 2 * pos + b

        def gather(s, _):
            first = s == 0
            lev = jnp.where(first, pos, jnp.minimum(s - 1, pos))
            m = jnp.where(first, b, mask_ref[own, 2 * lev + 1])
            cnt = jnp.where(m == 1, count_ref[2 * lev + 1], count_ref[2 * lev])
            cnt = jnp.where(s < nl, cnt, 0)
            ks = pl.ds(pl.multiple_of(s * BLOCK, BLOCK), BLOCK)
            kx[ks, 0:128] = jnp.where(m == 1, ka[lev, 128:256], ka[lev, 0:128])
            vx[ks, 0:128] = jnp.where(m == 1, va[lev, 128:256], va[lev, 0:128])
            bias = jnp.where(sub < cnt, 0.0, NEG)
            kx[ks, 128:256] = jnp.where(lane == 0, bias, 0.0).astype(bf16)
            vx[ks, 128:256] = jnp.where(lane < 3, -1.0, 0.0).astype(bf16)
            return 0

        lax.fori_loop(0, nch * LC, gather, 0)
        ml[0:1, :] = jnp.full((1, R), NEG, f32)
        ml[1:2, :] = jnp.zeros((1, R), f32)

        def pass1(c, first):
            ks = chunk(c)
            kc = kx[ks, :]
            for r in range(NRT):
                rs = slice(r * RT, (r + 1) * RT)
                s = dot(kc, qT[b, :, rs])
                if first:
                    s = jnp.concatenate([s[0:BLOCK] + causal, s[BLOCK:]], axis=0)
                s_scr[ks, rs] = s
                old = ml[0:1, rs]
                new = jnp.maximum(old, jnp.max(s, axis=0, keepdims=True))
                e = jnp.exp2((s - new) * C2)
                ml[1:2, rs] = ml[1:2, rs] * jnp.exp2((old - new) * C2) + jnp.sum(e, axis=0, keepdims=True)
                ml[0:1, rs] = new

        pass1(0, True)

        def later(c, _):
            pass1(c, False)
            return 0

        lax.fori_loop(1, nch, later, 0)
        ml[2:3, :] = ml[0:1, :] * C2 + jnp.log2(ml[1:2, :])
        ot[...] = jnp.zeros_like(ot)
        dqt[...] = jnp.zeros_like(dqt)

        def forward(c, _):
            ks = chunk(c)
            vc = vx[ks, 0:128]
            acc = None
            for r in range(NRT):
                rs = slice(r * RT, (r + 1) * RT)
                p = jnp.exp2(s_scr[ks, rs] * C2 - ml[2:3, rs])
                s_scr[ks, rs] = p
                low = p.astype(bf16)
                ot[:, rs] += dot_lhs_t(vc, low)
                t = dot(low, grows[b, rs, :])
                acc = t if acc is None else acc + t
            dv[b, ks, :] = acc
            return 0

        lax.fori_loop(0, nch, forward, 0)
        if b == 1:
            combine(dv, pv)
            scatter_leaves(z, y, 1, parts, land, ssem)
        olow = ot[...].astype(bf16)
        delta = jnp.sum(olow.astype(f32) * gT[b, 0:128, :].astype(f32), axis=0, keepdims=True)
        d0 = delta.astype(bf16)
        r1 = delta - d0.astype(f32)
        d1 = r1.astype(bf16)
        d2 = (r1 - d1.astype(f32)).astype(bf16)
        pieces = jnp.where(extra == 0, d0.astype(f32), jnp.where(extra == 1, d1.astype(f32), jnp.where(extra == 2, d2.astype(f32), 0.0)))
        gT[b, 128:256, :] = pieces.astype(bf16)
        rows = pl.ds(b * BLOCK, BLOCK)
        for i in range(HEADS):
            hs = slice(i * 128, (i + 1) * 128)
            o_scr[rows, hs] = olow[:, hs].T

        def backward(c, _):
            ks = chunk(c)
            vc = vx[ks, :]
            kc = kx[ks, 0:128]
            acc = None
            for r in range(NRT):
                rs = slice(r * RT, (r + 1) * RT)
                dp = dot(vc, gT[b, :, rs])
                ds = (s_scr[ks, rs] * dp).astype(bf16)
                dqt[:, rs] += dot_lhs_t(kc, ds)
                t = dot(ds, qrows[b, rs, :])
                acc = t if acc is None else acc + t
            acc = acc * SCALE
            dk[b, ks, :] = acc
            ml[3:4, 0:DH] += jnp.sum(acc * kc.astype(f32), axis=0, keepdims=True)
            return 0

        lax.fori_loop(0, nch, backward, 0)
        if b == 1:
            combine(dk, pk)
            scatter_leaves(z, y, 0, parts, land, ssem)
        for i in range(HEADS):
            hs = slice(i * 128, (i + 1) * 128)
            gqn = dqt[:, hs].T * SCALE
            hat, inv = normed(q_ref[rows, hs])
            gq_scr[rows, hs] = norm_backward(gqn, hat, inv, gain).astype(bf16)
            q_part = q_part + jnp.sum(gqn * hat, axis=0, keepdims=True)
    done = [pltpu.make_async_copy(o_scr, out_ref, lsem.at[0]), pltpu.make_async_copy(gq_scr, gq_ref, lsem.at[1])]
    for cp in done:
        cp.start()
    gains = jnp.concatenate([q_part, ml[3:4, 0:DH] / kg_ref[...], jnp.zeros((6, DH), f32)], axis=0)
    c1 = spread(arh, h, asem, 0, nh, lambda j: {"heads": lax.rem(h + j, nh)}, gains)
    inner_v = [x for x in SCATTER if x[0][0] == 1]
    inner_k = [x for x in SCATTER if x[0][0] == 0]
    for x in inner_v:
        scatter_inner(z, y, x, parts, land, ssem)
    c2 = spread(arz, z, asem, nh - 1, NZ, lambda j: {"depth": level(z, y, j, 0)}, collect(arh, nh, c1))
    for x in inner_k[:len(inner_k) // 2]:
        scatter_inner(z, y, x, parts, land, ssem)
    c3 = spread(ary, y, asem, nh + NZ - 2, NY, lambda j: {"depth": level(z, y, 0, j)}, collect(arz, NZ, c2))
    for x in inner_k[len(inner_k) // 2:]:
        scatter_inner(z, y, x, parts, land, ssem)
    gv_ref[...] = scatter_own(z, y, 1, parts, land, ssem).astype(bf16)
    k_hat, k_inv = normed(k_ref[...])
    gk_ref[...] = norm_backward(scatter_own(z, y, 0, parts, land, ssem), k_hat, k_inv, kg_ref[...]).astype(bf16)
    gain_ref[...] = collect(ary, NY, c3)
    for cp in c1 + c2 + c3:
        cp.wait_send()
    gather_drain(z, y, kv, gsem)
    scatter_drain(z, y, parts, land, ssem)
    for cp in done:
        cp.wait()


def fused(mask, count, q, g, k, v, qg, kg, nh, LC=16, RT=256):
    vmem = pl.BlockSpec(memory_space=pltpu.VMEM)
    smem = pl.BlockSpec(memory_space=pltpu.SMEM)
    hbm = pl.BlockSpec(memory_space=pl.ANY)
    sd = jax.ShapeDtypeStruct
    na = nh + NZ + NY - 3
    rows = k.shape[0]
    V = pltpu.VMEM
    dma = pltpu.SemaphoreType.DMA
    return pl.pallas_call(
        functools.partial(fused_kernel, nh, LC, RT),
        out_shape=(sd(q.shape, bf16), sd(q.shape, bf16), sd(k.shape, bf16), sd(k.shape, bf16), sd((8, DH), f32)),
        in_specs=[smem, smem] + [vmem] * 6,
        out_specs=(hbm, hbm, vmem, vmem, vmem),
        scratch_shapes=[
            V((LEVELS, rows, DH), bf16), V((LEVELS, rows, DH), bf16), V((KT, 256), bf16), V((KT, 256), bf16), V((KT, R), f32),
            V((2, 256, R), bf16), V((2, 256, R), bf16), V((2, R, DH), bf16), V((2, R, DH), bf16),
            V((DH, R), f32), V((DH, R), f32), V((2, KT, DH), f32), V((2, KT, DH), f32), V((8, R), f32),
            V((LEVELS, rows, DH), bf16), V((LEVELS, rows, DH), bf16), V((NPIECE, rows // HALVES, DH), bf16),
            V(q.shape, bf16), V(q.shape, bf16),
            V((nh, 8, DH), f32), V((NZ, 8, DH), f32), V((NY, 8, DH), f32),
        ] + [dma((NPIECE,))] * 4 + [dma((na,))] * 2 + [dma((2,))],
        compiler_params=pltpu.CompilerParams(collective_id=0, has_side_effects=True, vmem_limit_bytes=60 * 2**20),
        name="tree_attention",
    )(mask, count, q, g, k, v, qg, kg)


def hand_on_kernel(*refs):
    n = len(refs) // 2
    for i in range(n):
        refs[n + i][...] = refs[i][...]


def hand_on(arrays):
    vmem = pl.BlockSpec(memory_space=pltpu.VMEM)
    n = len(arrays)
    return pl.pallas_call(
        hand_on_kernel,
        out_shape=tuple(jax.ShapeDtypeStruct(a.shape, a.dtype) for a in arrays),
        in_specs=[vmem] * n,
        out_specs=(vmem,) * n,
        name="hand_on",
    )(*arrays)


def body(q_raw, k_raw, values, q_gain, k_gain, grad_out, block_mask, block_count):
    out, gq, gk, gv, gains = fused(
        block_mask, block_count, q_raw, grad_out, k_raw, values,
        q_gain.reshape(1, DH), k_gain.reshape(1, DH), lax.axis_size("heads"),
    )
    out, gq, gk, gv, gains = hand_on((out, gq, gk, gv, gains))
    return out, gq, gk, gv, gains[0], gains[1]


def solution(mesh):
    rows = P("depth", "heads")
    return jax.shard_map(
        body,
        mesh=mesh,
        in_specs=(rows, rows, rows, P(), P(), rows, P(), P()),
        out_specs=(rows, rows, rows, rows, P(), P()),
        check_vma=False,
    )
```

```python
import functools
import math

import jax
import jax.numpy as jnp
from jax import lax
from jax.experimental import pallas as pl
from jax.experimental.pallas import tpu as pltpu
from jax.sharding import PartitionSpec as P

f32 = jnp.float32
bf16 = jnp.bfloat16
MESH = pl.DeviceIdType.MESH
DH = 128
BLOCK = 128
EPS = 1e-6
SCALE = DH ** -0.5
C2 = SCALE * math.log2(math.e)
NEG = -1e30
NZ, NY = 8, 4
HALVES = 2
LATENCY = 2.0*HALVES

STEP = {"z+": (1, 0), "z-": (-1, 0), "y+": (0, 1), "y-": (0, -1)}
BACK = {"z+": "z-", "z-": "z+", "y+": "y-", "y-": "y+"}
PARTS = [(t, s) for t in range(2) for s in range(HALVES)]


def build_trees():
    parent = {}
    for part in PARTS:
        z_last = (part[1] if HALVES == 2 else part[0]) == 0
        for oz in range(NZ):
            for oy in range(NY):
                if (oz, oy) == (0, 0):
                    continue
                zdir = "z+" if oz > NZ // 2 else "z-"
                ydir = {3: "y+", 1: "y-"}.get(oy)
                if z_last:
                    if oz == 0:
                        d = ydir or "y+"
                    elif oy == 2 and oz % 2 == 1:
                        d = "y+" if oz in (1, 5) else "y-"
                    elif oz == NZ // 2:
                        d = "z+" if oy in (0, 2) else "z-"
                    else:
                        d = zdir
                elif oy == 0:
                    d = "z+" if oz == NZ // 2 else zdir
                else:
                    d = ydir or ("y+" if oz % 2 == 0 else "y-")
                parent[part, oz, oy] = d
    children = {}
    for (part, oz, oy), d in parent.items():
        sz, sy = STEP[d]
        children.setdefault((part, (oz + sz) % NZ, (oy + sy) % NY), []).append((d, (part, oz, oy)))
    return parent, children


PARENT, CHILDREN = build_trees()


def height(x):
    return 1 + max([height(c) for _, c in CHILDREN.get(x, [])], default=0)


def hops(x):
    part, oz, oy = x
    if (oz, oy) == (0, 0):
        return 0
    sz, sy = STEP[PARENT[x]]
    return 1 + hops((part, (oz + sz) % NZ, (oy + sy) % NY))


def needed_planes(x):
    part, oz, oy = x
    offsets = {0}
    stack = [(x, 0)]
    while stack:
        node, dz = stack.pop()
        offsets.add(dz)
        for d, c in CHILDREN.get(node, []):
            stack.append((c, dz + STEP[d][0]))
    return frozenset(z for z in range(NZ) if any((z + dz) % NZ >= (z + oz) % NZ for dz in offsets))


def gather_order():
    waiting, order, count, now = [], [], 0, 0
    free = dict.fromkeys(STEP, 0.0)
    def push(x, at):
        nonlocal count
        for d, c in CHILDREN.get(x, []):
            waiting.append((at, (-height(c), count), d, c))
            count += 1
    for part in PARTS:
        push((part, 0, 0), 0.0)
    done = []
    while waiting:
        start, key, d, c = min((max(free[w[2]], w[0]), w[1], w[2], w[3]) for w in waiting)
        waiting = [w for w in waiting if w[3] != c]
        free[d] = start + 1
        done.append((start + 1 + LATENCY, key, c))
        push(c, start + 1 + LATENCY)
    done.sort()
    return [(c, t) for t, _, c in done]


def scatter_order(lead):
    free = dict.fromkeys(STEP, -lead)
    arrived, order = {}, []
    left = set(PARENT)
    while left:
        best = None
        for x in left:
            kids = CHILDREN.get(x, [])
            if any(c not in arrived for _, c in kids):
                continue
            ready = max([arrived[c] for _, c in kids], default=-lead if x[0][0] == 1 else 0.0)
            d = BACK[PARENT[x]]
            key = (max(free[d], ready), -hops(x), PARTS.index(x[0]), x[1], x[2])
            if best is None or key < best[0]:
                best = (key, x, d)
        key, x, d = best
        left.remove(x)
        free[d] = key[0] + 1
        arrived[x] = key[0] + 1 + LATENCY
        order.append(x)
    return order


GATHER = [x for x, _ in gather_order()]
SCATTER = scatter_order(0.0)
INDEX = {x: i for i, x in enumerate(GATHER)}
PLANES = {x: needed_planes(x) for x in GATHER}
NPIECE = len(GATHER)


def level(z, y, oz, oy):
    return lax.rem(z + oz + NZ, NZ) * NY + lax.rem(y + oy + NY, NY)


def toward(z, y, d):
    return {"depth": level(z, y, *STEP[d])}


def among(z, planes):
    if len(planes) == NZ:
        return None
    return functools.reduce(jnp.logical_or, [z == p for p in sorted(planes)]) if planes else False


def guarded(cond, fn):
    if cond is None:
        fn()
    elif cond is not False:
        pl.when(cond)(fn)


def shifted(planes, d):
    return frozenset((p - STEP[d][0]) % NZ for p in planes)


def half(ref, lev, part):
    rows = ref.shape[1] // HALVES
    return ref.at[lev, pl.ds(part[1] * rows, rows)]


def copy_to(src, dst, send_sem, recv_sem, i, dev):
    return pltpu.make_async_remote_copy(src_ref=src, dst_ref=dst, send_sem=send_sem.at[i], recv_sem=recv_sem.at[i], device_id=dev, device_id_type=MESH)


def gather_piece(z, y, x, bufs, sems):
    part, oz, oy = x
    ref = half(bufs[part[0]], level(z, y, oz, oy), part)
    return copy_to(ref, ref, *sems, INDEX[x], toward(z, y, "z+"))


def gather_sends(z, y, x, bufs, sems, go):
    part, oz, oy = x
    for d, c in CHILDREN.get(x, []):
        ref = half(bufs[part[0]], level(z, y, oz, oy), part)
        cp = copy_to(ref, ref, *sems, INDEX[c], toward(z, y, d))
        guarded(among(z, shifted(PLANES[c], d)), cp.start if go else cp.wait_send)


def gather_own(z, y, bufs, sems):
    for part in PARTS:
        gather_sends(z, y, (part, 0, 0), bufs, sems, True)


def gather_rest(z, y, bufs, sems, pieces):
    for x in pieces:
        def step(x=x):
            gather_piece(z, y, x, bufs, sems).wait_recv()
            gather_sends(z, y, x, bufs, sems, True)
        guarded(among(z, PLANES[x]), step)


def gather_drain(z, y, bufs, sems):
    for part in PARTS:
        gather_sends(z, y, (part, 0, 0), bufs, sems, False)
    for x in GATHER:
        gather_sends(z, y, x, bufs, sems, False)


def leaf_planes(x):
    out = set(PLANES[x])
    for d, c in CHILDREN.get(x, []):
        out -= shifted(PLANES[c], d)
    return frozenset(out)


def scatter_send(z, y, x, bufs, land, sems):
    part, oz, oy = x
    return copy_to(half(bufs[part[0]], level(z, y, oz, oy), part), land.at[INDEX[x]], *sems, INDEX[x], toward(z, y, BACK[PARENT[x]]))


def scatter_leaves(z, y, tensor, bufs, land, sems, chosen=None):
    for x in SCATTER:
        planes = leaf_planes(x)
        if planes and x[0][0] == tensor:
            cond = among(z, planes)
            if chosen is not None:
                pick = chosen(level(z, y, x[1], x[2]))
                cond = pick if cond is None else jnp.logical_and(cond, pick)
            guarded(cond, lambda x=x: scatter_send(z, y, x, bufs, land, sems).start())


def scatter_total(z, y, x, bufs, land, sems):
    part, oz, oy = x
    total = half(bufs[part[0]], level(z, y, oz, oy), part)
    kids = [c for d, c in CHILDREN.get(x, [])]
    for d, c in CHILDREN.get(x, []):
        i = INDEX[c]
        arrival = copy_to(land.at[i], land.at[i], *sems, i, toward(z, y, "z+"))
        guarded(among(z, shifted(PLANES[c], d)), arrival.wait_recv)
    total = total[...].astype(f32)
    for c in kids:
        total = total + land[INDEX[c]].astype(f32)
    return total


def scatter_inner(z, y, x, bufs, land, sems):
    part, oz, oy = x
    def step():
        half(bufs[part[0]], level(z, y, oz, oy), part)[...] = scatter_total(z, y, x, bufs, land, sems).astype(bf16)
        scatter_send(z, y, x, bufs, land, sems).start()
    guarded(among(z, PLANES[x] - leaf_planes(x)), step)


def scatter_own(z, y, tensor, bufs, land, sems):
    return jnp.concatenate([scatter_total(z, y, (part, 0, 0), bufs, land, sems) for part in PARTS if part[0] == tensor], axis=0)


def scatter_drain(z, y, bufs, land, sems):
    for x in SCATTER:
        guarded(among(z, PLANES[x]), lambda x=x: scatter_send(z, y, x, bufs, land, sems).wait_send())


def spread(buf, mine, sems, base, n, device, part):
    buf[mine] = part
    copies = []
    for j in range(1, n):
        cp = copy_to(buf.at[mine], buf.at[mine], *sems, base + j - 1, device(j))
        cp.start()
        copies.append(cp)
    return copies


def collect(buf, n, copies):
    for cp in copies:
        cp.wait_recv()
    total = buf[0]
    for j in range(1, n):
        total = total + buf[j]
    return total


def greet(z, y, h, nh):
    peers = [{"heads": lax.rem(h + j, nh)} for j in range(1, nh)]
    peers += [{"depth": level(z, y, j, 0)} for j in range(1, NZ)]
    peers += [{"depth": level(z, y, 0, j)} for j in range(1, NY)]
    bar = pltpu.get_barrier_semaphore()
    for d in peers:
        pl.semaphore_signal(bar, inc=1, device_id=d, device_id_type=MESH)
    return lambda: pl.semaphore_wait(bar, len(peers))

LEVELS = NZ * NY
HEADS = 8
R = HEADS * BLOCK
KT = LEVELS * BLOCK


def dot(a, b):
    return jnp.dot(a, b, preferred_element_type=f32)


def dot_lhs_t(a, b):
    return lax.dot_general(a, b, (((0,), (0,)), ((), ())), preferred_element_type=f32)


def normed(rows):
    x = rows.astype(f32)
    inv = 1.0 / jnp.sqrt(jnp.mean(x * x, axis=-1, keepdims=True) + EPS)
    return x * inv, inv


def norm_backward(grad, hat, inv, gain):
    gh = grad * gain
    return inv * (gh - hat * jnp.mean(gh * hat, axis=-1, keepdims=True))


def fused_kernel(nh, LC, RT, mask_ref, count_ref, q_ref, g_ref, k_ref, v_ref, qg_ref, kg_ref,
                 out_ref, gq_ref, gk_ref, gv_ref, qgain_ref, kgain_ref,
                 ka, va, kx, vx, s_scr, qT, gT, qrows, grows, ot, dqt, dk, dv, ml, pk, pv, land, o_scr, gq_scr,
                 arh, arz, ary, gsend, grecv, ssend, srecv, asend, arecv, lsem):
    pos = lax.axis_index("depth")
    h = lax.axis_index("heads")
    z, y = pos // NY, pos % NY
    gsem, ssem, asem = (gsend, grecv), (ssend, srecv), (asend, arecv)
    kv, parts = (ka, va), (pk, pv)
    greeted = greet(z, y, h, nh)
    k_hat, k_inv = normed(k_ref[...])
    ka[pos] = (k_hat * kg_ref[...]).astype(bf16)
    va[pos] = v_ref[...]
    land[...] = jnp.zeros_like(land)
    greeted()
    gather_own(z, y, kv, gsem)

    nl = pos + 1
    nch = (nl + LC - 1) // LC
    CK = LC * BLOCK
    NRT = R // RT
    gain = qg_ref[...]
    lane = lax.broadcasted_iota(jnp.int32, (BLOCK, BLOCK), 1)
    sub = lax.broadcasted_iota(jnp.int32, (BLOCK, BLOCK), 0)
    causal = jnp.where(sub <= lane, 0.0, NEG).astype(f32)
    causal = jnp.concatenate([causal] * (RT // BLOCK), axis=1)
    extra = lax.broadcasted_iota(jnp.int32, (BLOCK, R), 0)

    def prepare(b):
        rows = pl.ds(b * BLOCK, BLOCK)
        qT[b, 128:256, :] = jnp.where(extra == 0, 1.0, 0.0).astype(bf16)
        for i in range(HEADS):
            hs = slice(i * 128, (i + 1) * 128)
            hat, inv = normed(q_ref[rows, hs])
            low = (hat * gain).astype(bf16)
            qrows[b, hs, :] = low
            qT[b, 0:128, hs] = low.T
            gr = g_ref[rows, hs]
            grows[b, hs, :] = gr
            gT[b, 0:128, hs] = gr.T

    prepare(0)

    def fill(i, _):
        pk[i] = jnp.zeros((2 * BLOCK, DH), bf16)
        pv[i] = jnp.zeros((2 * BLOCK, DH), bf16)
        return 0

    lax.fori_loop(NY * (z + 1), LEVELS, fill, 0)
    gather_rest(z, y, kv, gsem, GATHER[:NPIECE // 3])
    prepare(1)
    gather_rest(z, y, kv, gsem, GATHER[NPIECE // 3:])

    def tile(c, t):
        size = NY * BLOCK
        return pl.ds(pl.multiple_of(c * CK + t * size, size), size)

    def chunk(c):
        return pl.ds(pl.multiple_of(c * CK, CK), CK)

    def combine(src, dst, start, stop):
        def one(i):
            ks = pl.ds(pl.multiple_of(jnp.minimum(i + 1, LEVELS - 1) * BLOCK, BLOCK), BLOCK)
            m0 = mask_ref[2 * pos, 2 * i + 1]
            m1 = mask_ref[2 * pos + 1, 2 * i + 1]
            a0 = jnp.where(i < pos, src[0, ks, :], 0.0)
            a1 = jnp.where(i < pos, src[1, ks, :], 0.0)
            for m in range(2):
                both = jnp.where(m0 == m, a0, 0.0) + jnp.where(m1 == m, a1, 0.0)
                dst[i, m * BLOCK:(m + 1) * BLOCK, :] = both.astype(bf16)

        def four(i, _):
            for t in range(4):
                one(4 * i + t)
            return 0

        lax.fori_loop(jnp.maximum(start, 0), stop, four, 0)
        def own_level():
            for b in range(2):
                dst[pos, b * BLOCK:(b + 1) * BLOCK, :] = src[b, 0:BLOCK, :].astype(bf16)

        pl.when(stop == z + 1)(own_level)

    q_part = jnp.zeros((1, DH), f32)
    ml[3:4, 0:DH] = jnp.zeros((1, DH), f32)
    for b in range(2):
        own = 2 * pos + b

        def gather_slot(s):
            first = s == 0
            lev = jnp.where(first, pos, jnp.minimum(s - 1, pos))
            m = jnp.where(first, b, mask_ref[own, 2 * lev + 1])
            cnt = jnp.where(m == 1, count_ref[2 * lev + 1], count_ref[2 * lev])
            cnt = jnp.where(s < nl, cnt, 0)
            ks = pl.ds(pl.multiple_of(s * BLOCK, BLOCK), BLOCK)
            kx[ks, 0:128] = jnp.where(m == 1, ka[lev, 128:256], ka[lev, 0:128])
            vx[ks, 0:128] = jnp.where(m == 1, va[lev, 128:256], va[lev, 0:128])
            bias = jnp.where(sub < cnt, 0.0, NEG)
            kx[ks, 128:256] = jnp.where(lane == 0, bias, 0.0).astype(bf16)
            if b == 0:
                vx[ks, 128:256] = jnp.where(lane < 3, -1.0, 0.0).astype(bf16)

        def gather(i, _):
            for t in range(4):
                gather_slot(4 * i + t)
            return 0

        lax.fori_loop(0, nch * (LC // 4), gather, 0)
        ml[0:1, :] = jnp.full((1, R), NEG, f32)
        ml[1:2, :] = jnp.zeros((1, R), f32)

        def pass1(c, first):
            ks = chunk(c)
            kc = kx[ks, :]
            for r in range(NRT):
                rs = slice(r * RT, (r + 1) * RT)
                s = dot(kc, qT[b, :, rs])
                if first:
                    s = jnp.concatenate([s[0:BLOCK] + causal, s[BLOCK:]], axis=0)
                s_scr[ks, rs] = s
                old = ml[0:1, rs]
                new = jnp.maximum(old, jnp.max(s, axis=0, keepdims=True))
                e = jnp.exp2((s - new) * C2)
                ml[1:2, rs] = ml[1:2, rs] * jnp.exp2((old - new) * C2) + jnp.sum(e, axis=0, keepdims=True)
                ml[0:1, rs] = new

        pass1(0, True)

        def later(c, _):
            pass1(c, False)
            return 0

        lax.fori_loop(1, nch, later, 0)
        ml[2:3, :] = ml[0:1, :] * C2 + jnp.log2(ml[1:2, :])
        ot[...] = jnp.zeros_like(ot)
        dqt[...] = jnp.zeros_like(dqt)

        def forward(c, _):
            for t in range(LC // NY):
                ks = tile(c, t)
                p = jnp.exp2(s_scr[ks, :] * C2 - ml[2:3, :])
                s_scr[ks, :] = p
                low = p.astype(bf16)
                ot[...] += dot_lhs_t(vx[ks, 0:128], low)
                dv[b, ks, :] = dot(low, grows[b])
            return 0

        lax.fori_loop(0, nch, forward, 0)
        if b == 1:
            combine(dv, pv, 0, z + 1)
            scatter_leaves(z, y, 1, parts, land, ssem)
        olow = ot[...].astype(bf16)
        delta = jnp.sum(olow.astype(f32) * gT[b, 0:128, :].astype(f32), axis=0, keepdims=True)
        d0 = delta.astype(bf16)
        r1 = delta - d0.astype(f32)
        d1 = r1.astype(bf16)
        d2 = (r1 - d1.astype(f32)).astype(bf16)
        pieces = jnp.where(extra == 0, d0.astype(f32), jnp.where(extra == 1, d1.astype(f32), jnp.where(extra == 2, d2.astype(f32), 0.0)))
        gT[b, 128:256, :] = pieces.astype(bf16)
        rows = pl.ds(b * BLOCK, BLOCK)
        for i in range(HEADS):
            hs = slice(i * 128, (i + 1) * 128)
            o_scr[rows, hs] = olow[:, hs].T

        def backward(c, _):
            for t in range(LC // NY):
                ks = tile(c, t)
                kc = kx[ks, 0:128]
                dp = dot(vx[ks, :], gT[b])
                ds = (s_scr[ks, :] * dp).astype(bf16)
                dqt[...] += dot_lhs_t(kc, ds)
                acc = dot(ds, qrows[b]) * SCALE
                dk[b, ks, :] = acc
                ml[3:4, 0:DH] += jnp.sum(acc * kc.astype(f32), axis=0, keepdims=True)
            return 0

        if b == 0:
            lax.fori_loop(0, nch, backward, 0)
        else:
            early = (nch - 1) * (LC // NY - 1)
            lax.fori_loop(0, nch - 1, backward, 0)
            combine(dk, pk, 0, early)
            scatter_leaves(z, y, 0, parts, land, ssem, lambda lev: lev < NY * early)
            lax.fori_loop(nch - 1, nch, backward, 0)
            combine(dk, pk, early, z + 1)
            scatter_leaves(z, y, 0, parts, land, ssem, lambda lev: lev >= NY * early)
        for i in range(HEADS):
            hs = slice(i * 128, (i + 1) * 128)
            gqn = dqt[:, hs].T * SCALE
            hat, inv = normed(q_ref[rows, hs])
            gq_scr[rows, hs] = norm_backward(gqn, hat, inv, gain).astype(bf16)
            q_part = q_part + jnp.sum(gqn * hat, axis=0, keepdims=True)
    done = [pltpu.make_async_copy(o_scr, out_ref, lsem.at[0]), pltpu.make_async_copy(gq_scr, gq_ref, lsem.at[1])]
    for cp in done:
        cp.start()
    gains = jnp.concatenate([q_part, ml[3:4, 0:DH] / kg_ref[...], jnp.zeros((6, DH), f32)], axis=0)
    c1 = spread(arh, h, asem, 0, nh, lambda j: {"heads": lax.rem(h + j, nh)}, gains)
    third = len(SCATTER) // 3
    for x in SCATTER[:third]:
        scatter_inner(z, y, x, parts, land, ssem)
    c2 = spread(arz, z, asem, nh - 1, NZ, lambda j: {"depth": level(z, y, j, 0)}, collect(arh, nh, c1))
    for x in SCATTER[third:2 * third]:
        scatter_inner(z, y, x, parts, land, ssem)
    c3 = spread(ary, y, asem, nh + NZ - 2, NY, lambda j: {"depth": level(z, y, 0, j)}, collect(arz, NZ, c2))
    for x in SCATTER[2 * third:]:
        scatter_inner(z, y, x, parts, land, ssem)
    gv_ref[...] = scatter_own(z, y, 1, parts, land, ssem).astype(bf16)
    k_hat, k_inv = normed(k_ref[...])
    gk_ref[...] = norm_backward(scatter_own(z, y, 0, parts, land, ssem), k_hat, k_inv, kg_ref[...]).astype(bf16)
    total = collect(ary, NY, c3)
    qgain_ref[...] = total[0:1]
    kgain_ref[...] = total[1:2]
    for cp in c1 + c2 + c3:
        cp.wait_send()
    gather_drain(z, y, kv, gsem)
    scatter_drain(z, y, parts, land, ssem)
    for cp in done:
        cp.wait()


def fused(mask, count, q, g, k, v, qg, kg, nh, LC=16, RT=256):
    vmem = pl.BlockSpec(memory_space=pltpu.VMEM)
    smem = pl.BlockSpec(memory_space=pltpu.SMEM)
    hbm = pl.BlockSpec(memory_space=pl.ANY)
    sd = jax.ShapeDtypeStruct
    na = nh + NZ + NY - 3
    rows = k.shape[0]
    V = pltpu.VMEM
    dma = pltpu.SemaphoreType.DMA
    return pl.pallas_call(
        functools.partial(fused_kernel, nh, LC, RT),
        out_shape=(sd(q.shape, bf16), sd(q.shape, bf16), sd(k.shape, bf16), sd(k.shape, bf16), sd((1, DH), f32), sd((1, DH), f32)),
        in_specs=[smem, smem] + [vmem] * 6,
        out_specs=(hbm, hbm, vmem, vmem, vmem, vmem),
        scratch_shapes=[
            V((LEVELS, rows, DH), bf16), V((LEVELS, rows, DH), bf16), V((KT, 256), bf16), V((KT, 256), bf16), V((KT, R), f32),
            V((2, 256, R), bf16), V((2, 256, R), bf16), V((2, R, DH), bf16), V((2, R, DH), bf16),
            V((DH, R), f32), V((DH, R), f32), V((2, KT, DH), f32), V((2, KT, DH), f32), V((8, R), f32),
            V((LEVELS, rows, DH), bf16), V((LEVELS, rows, DH), bf16), V((NPIECE, rows // HALVES, DH), bf16),
            V(q.shape, bf16), V(q.shape, bf16),
            V((nh, 8, DH), f32), V((NZ, 8, DH), f32), V((NY, 8, DH), f32),
        ] + [dma((NPIECE,))] * 4 + [dma((na,))] * 2 + [dma((2,))],
        compiler_params=pltpu.CompilerParams(collective_id=0, has_side_effects=True, vmem_limit_bytes=60 * 2**20),
        name="tree_attention",
    )(mask, count, q, g, k, v, qg, kg)


def hand_on_kernel(*refs):
    n = len(refs) // 2
    for i in range(n):
        refs[n + i][...] = refs[i][...]


def hand_on(arrays):
    vmem = pl.BlockSpec(memory_space=pltpu.VMEM)
    n = len(arrays)
    return pl.pallas_call(
        hand_on_kernel,
        out_shape=tuple(jax.ShapeDtypeStruct(a.shape, a.dtype) for a in arrays),
        in_specs=[vmem] * n,
        out_specs=(vmem,) * n,
        name="hand_on",
    )(*arrays)


def body(q_raw, k_raw, values, q_gain, k_gain, grad_out, block_mask, block_count):
    results = fused(
        block_mask, block_count, q_raw, grad_out, k_raw, values,
        q_gain.reshape(1, DH), k_gain.reshape(1, DH), lax.axis_size("heads"),
    )
    out, gq, gk, gv, q_part, k_part = hand_on(results)
    return out, gq, gk, gv, q_part.reshape(DH), k_part.reshape(DH)


def solution(mesh):
    rows = P("depth", "heads")
    return jax.shard_map(
        body,
        mesh=mesh,
        in_specs=(rows, rows, rows, P(), P(), rows, P(), P()),
        out_specs=(rows, rows, rows, rows, P(), P()),
        check_vma=False,
    )
```

```python
import functools
import math

import jax
import jax.numpy as jnp
from jax import lax
from jax.experimental import pallas as pl
from jax.experimental.pallas import tpu as pltpu
from jax.sharding import PartitionSpec as P

f32 = jnp.float32
bf16 = jnp.bfloat16
MESH = pl.DeviceIdType.MESH
DH = 128
BLOCK = 128
EPS = 1e-6
SCALE = DH ** -0.5
C2 = SCALE * math.log2(math.e)
NEG = -1e30
NZ, NY = 8, 4
HALVES = 2
LATENCY = 2.0*HALVES

STEP = {"z+": (1, 0), "z-": (-1, 0), "y+": (0, 1), "y-": (0, -1)}
BACK = {"z+": "z-", "z-": "z+", "y+": "y-", "y-": "y+"}
PARTS = [(t, s) for t in range(2) for s in range(HALVES)]


def build_trees():
    parent = {}
    for part in PARTS:
        z_last = (part[1] if HALVES == 2 else part[0]) == 0
        for oz in range(NZ):
            for oy in range(NY):
                if (oz, oy) == (0, 0):
                    continue
                zdir = "z+" if oz > NZ // 2 else "z-"
                ydir = {3: "y+", 1: "y-"}.get(oy)
                if z_last:
                    if oz == 0:
                        d = ydir or "y+"
                    elif oy == 2 and oz % 2 == 1:
                        d = "y+" if oz in (1, 5) else "y-"
                    elif oz == NZ // 2:
                        d = "z+" if oy in (0, 2) else "z-"
                    else:
                        d = zdir
                elif oy == 0:
                    d = "z+" if oz == NZ // 2 else zdir
                else:
                    d = ydir or ("y+" if oz % 2 == 0 else "y-")
                parent[part, oz, oy] = d
    children = {}
    for (part, oz, oy), d in parent.items():
        sz, sy = STEP[d]
        children.setdefault((part, (oz + sz) % NZ, (oy + sy) % NY), []).append((d, (part, oz, oy)))
    return parent, children


PARENT, CHILDREN = build_trees()


def height(x):
    return 1 + max([height(c) for _, c in CHILDREN.get(x, [])], default=0)


def hops(x):
    part, oz, oy = x
    if (oz, oy) == (0, 0):
        return 0
    sz, sy = STEP[PARENT[x]]
    return 1 + hops((part, (oz + sz) % NZ, (oy + sy) % NY))


def needed_planes(x):
    part, oz, oy = x
    offsets = {0}
    stack = [(x, 0)]
    while stack:
        node, dz = stack.pop()
        offsets.add(dz)
        for d, c in CHILDREN.get(node, []):
            stack.append((c, dz + STEP[d][0]))
    return frozenset(z for z in range(NZ) if any((z + dz) % NZ >= (z + oz) % NZ for dz in offsets))


def gather_order():
    waiting, order, count, now = [], [], 0, 0
    free = dict.fromkeys(STEP, 0.0)
    def push(x, at):
        nonlocal count
        for d, c in CHILDREN.get(x, []):
            waiting.append((at, (-height(c), count), d, c))
            count += 1
    for part in PARTS:
        push((part, 0, 0), 0.0)
    done = []
    while waiting:
        start, key, d, c = min((max(free[w[2]], w[0]), w[1], w[2], w[3]) for w in waiting)
        waiting = [w for w in waiting if w[3] != c]
        free[d] = start + 1
        done.append((start + 1 + LATENCY, key, c))
        push(c, start + 1 + LATENCY)
    done.sort()
    return [(c, t) for t, _, c in done]


def scatter_order(lead):
    free = dict.fromkeys(STEP, -lead)
    arrived, order = {}, []
    left = set(PARENT)
    while left:
        best = None
        for x in left:
            kids = CHILDREN.get(x, [])
            if any(c not in arrived for _, c in kids):
                continue
            ready = max([arrived[c] for _, c in kids], default=-lead if x[0][0] == 1 else 0.0)
            d = BACK[PARENT[x]]
            key = (max(free[d], ready), -hops(x), PARTS.index(x[0]), x[1], x[2])
            if best is None or key < best[0]:
                best = (key, x, d)
        key, x, d = best
        left.remove(x)
        free[d] = key[0] + 1
        arrived[x] = key[0] + 1 + LATENCY
        order.append(x)
    return order


GATHER = [x for x, _ in gather_order()]
SCATTER = scatter_order(0.0)
INDEX = {x: i for i, x in enumerate(GATHER)}
PLANES = {x: needed_planes(x) for x in GATHER}
NPIECE = len(GATHER)


def level(z, y, oz, oy):
    return lax.rem(z + oz + NZ, NZ) * NY + lax.rem(y + oy + NY, NY)


def toward(z, y, d):
    return {"depth": level(z, y, *STEP[d])}


def among(z, planes):
    if len(planes) == NZ:
        return None
    return functools.reduce(jnp.logical_or, [z == p for p in sorted(planes)]) if planes else False


def guarded(cond, fn):
    if cond is None:
        fn()
    elif cond is not False:
        pl.when(cond)(fn)


def shifted(planes, d):
    return frozenset((p - STEP[d][0]) % NZ for p in planes)


def half(ref, lev, part):
    rows = ref.shape[1] // HALVES
    return ref.at[lev, pl.ds(part[1] * rows, rows)]


def copy_to(src, dst, send_sem, recv_sem, i, dev):
    return pltpu.make_async_remote_copy(src_ref=src, dst_ref=dst, send_sem=send_sem.at[i], recv_sem=recv_sem.at[i], device_id=dev, device_id_type=MESH)


def gather_piece(z, y, x, bufs, sems):
    part, oz, oy = x
    ref = half(bufs[part[0]], level(z, y, oz, oy), part)
    return copy_to(ref, ref, *sems, INDEX[x], toward(z, y, "z+"))


def gather_sends(z, y, x, bufs, sems, go):
    part, oz, oy = x
    for d, c in CHILDREN.get(x, []):
        ref = half(bufs[part[0]], level(z, y, oz, oy), part)
        cp = copy_to(ref, ref, *sems, INDEX[c], toward(z, y, d))
        guarded(among(z, shifted(PLANES[c], d)), cp.start if go else cp.wait_send)


def gather_own(z, y, bufs, sems):
    for part in PARTS:
        gather_sends(z, y, (part, 0, 0), bufs, sems, True)


def gather_rest(z, y, bufs, sems, pieces):
    for x in pieces:
        def step(x=x):
            gather_piece(z, y, x, bufs, sems).wait_recv()
            gather_sends(z, y, x, bufs, sems, True)
        guarded(among(z, PLANES[x]), step)


def gather_drain(z, y, bufs, sems):
    for part in PARTS:
        gather_sends(z, y, (part, 0, 0), bufs, sems, False)
    for x in GATHER:
        gather_sends(z, y, x, bufs, sems, False)


def leaf_planes(x):
    out = set(PLANES[x])
    for d, c in CHILDREN.get(x, []):
        out -= shifted(PLANES[c], d)
    return frozenset(out)


def scatter_send(z, y, x, bufs, land, sems):
    part, oz, oy = x
    return copy_to(half(bufs[part[0]], level(z, y, oz, oy), part), land.at[INDEX[x]], *sems, INDEX[x], toward(z, y, BACK[PARENT[x]]))


def scatter_leaves(z, y, tensor, bufs, land, sems, chosen=None):
    for x in SCATTER:
        planes = leaf_planes(x)
        if planes and x[0][0] == tensor:
            cond = among(z, planes)
            if chosen is not None:
                pick = chosen(level(z, y, x[1], x[2]))
                cond = pick if cond is None else jnp.logical_and(cond, pick)
            guarded(cond, lambda x=x: scatter_send(z, y, x, bufs, land, sems).start())


def scatter_total(z, y, x, bufs, land, sems):
    part, oz, oy = x
    total = half(bufs[part[0]], level(z, y, oz, oy), part)
    kids = [c for d, c in CHILDREN.get(x, [])]
    for d, c in CHILDREN.get(x, []):
        i = INDEX[c]
        arrival = copy_to(land.at[i], land.at[i], *sems, i, toward(z, y, "z+"))
        guarded(among(z, shifted(PLANES[c], d)), arrival.wait_recv)
    total = total[...].astype(f32)
    for c in kids:
        total = total + land[INDEX[c]].astype(f32)
    return total


def scatter_inner(z, y, x, bufs, land, sems):
    part, oz, oy = x
    def step():
        half(bufs[part[0]], level(z, y, oz, oy), part)[...] = scatter_total(z, y, x, bufs, land, sems).astype(bf16)
        scatter_send(z, y, x, bufs, land, sems).start()
    guarded(among(z, PLANES[x] - leaf_planes(x)), step)


def scatter_own(z, y, tensor, bufs, land, sems):
    return jnp.concatenate([scatter_total(z, y, (part, 0, 0), bufs, land, sems) for part in PARTS if part[0] == tensor], axis=0)


def scatter_drain(z, y, bufs, land, sems):
    for x in SCATTER:
        guarded(among(z, PLANES[x]), lambda x=x: scatter_send(z, y, x, bufs, land, sems).wait_send())


def spread(buf, mine, sems, base, n, device, part):
    buf[mine] = part
    copies = []
    for j in range(1, n):
        cp = copy_to(buf.at[mine], buf.at[mine], *sems, base + j - 1, device(j))
        cp.start()
        copies.append(cp)
    return copies


def collect(buf, n, copies):
    for cp in copies:
        cp.wait_recv()
    total = buf[0]
    for j in range(1, n):
        total = total + buf[j]
    return total


def greet(z, y, h, nh):
    peers = [{"heads": lax.rem(h + j, nh)} for j in range(1, nh)]
    peers += [{"depth": level(z, y, j, 0)} for j in range(1, NZ)]
    peers += [{"depth": level(z, y, 0, j)} for j in range(1, NY)]
    bar = pltpu.get_barrier_semaphore()
    for d in peers:
        pl.semaphore_signal(bar, inc=1, device_id=d, device_id_type=MESH)
    return lambda: pl.semaphore_wait(bar, len(peers))

LEVELS = NZ * NY
HEADS = 8
R = HEADS * BLOCK
KT = LEVELS * BLOCK


def dot(a, b):
    return jnp.dot(a, b, preferred_element_type=f32)


def dot_lhs_t(a, b):
    return lax.dot_general(a, b, (((0,), (0,)), ((), ())), preferred_element_type=f32)


def normed(rows):
    x = rows.astype(f32)
    inv = 1.0 / jnp.sqrt(jnp.mean(x * x, axis=-1, keepdims=True) + EPS)
    return x * inv, inv


def norm_backward(grad, hat, inv, gain):
    gh = grad * gain
    return inv * (gh - hat * jnp.mean(gh * hat, axis=-1, keepdims=True))


def fused_kernel(nh, LC, RT, mask_ref, count_ref, q_ref, g_ref, k_ref, v_ref, qg_ref, kg_ref,
                 out_ref, gq_ref, gk_ref, gv_ref, qgain_ref, kgain_ref,
                 ka, va, kx, vx, s_scr, qT, gT, qrows, grows, ot, dqt, dk, dv, ml, pk, pv, land, o_scr, gq_scr,
                 arh, arz, ary, gsend, grecv, ssend, srecv, asend, arecv, lsem):
    pos = lax.axis_index("depth")
    h = lax.axis_index("heads")
    z, y = pos // NY, pos % NY
    gsem, ssem, asem = (gsend, grecv), (ssend, srecv), (asend, arecv)
    kv, parts = (ka, va), (pk, pv)
    greeted = greet(z, y, h, nh)
    k_hat, k_inv = normed(k_ref[...])
    ka[pos] = (k_hat * kg_ref[...]).astype(bf16)
    va[pos] = v_ref[...]
    land[...] = jnp.zeros_like(land)
    greeted()
    gather_own(z, y, kv, gsem)

    nl = pos + 1
    nch = (nl + LC - 1) // LC
    CK = LC * BLOCK
    NRT = R // RT
    gain = qg_ref[...]
    lane = lax.broadcasted_iota(jnp.int32, (BLOCK, BLOCK), 1)
    sub = lax.broadcasted_iota(jnp.int32, (BLOCK, BLOCK), 0)
    causal = jnp.where(sub <= lane, 0.0, NEG).astype(f32)
    causal = jnp.concatenate([causal] * (RT // BLOCK), axis=1)
    extra = lax.broadcasted_iota(jnp.int32, (BLOCK, R), 0)

    def prepare(b):
        rows = pl.ds(b * BLOCK, BLOCK)
        qT[b, 128:256, :] = jnp.where(extra == 0, 1.0, 0.0).astype(bf16)
        for i in range(HEADS):
            hs = slice(i * 128, (i + 1) * 128)
            hat, inv = normed(q_ref[rows, hs])
            low = (hat * gain).astype(bf16)
            qrows[b, hs, :] = low
            qT[b, 0:128, hs] = low.T
            gr = g_ref[rows, hs]
            grows[b, hs, :] = gr
            gT[b, 0:128, hs] = gr.T


    def fill(i, _):
        pk[i] = jnp.zeros((2 * BLOCK, DH), bf16)
        pv[i] = jnp.zeros((2 * BLOCK, DH), bf16)
        return 0

    lax.fori_loop(NY * (z + 1), LEVELS, fill, 0)
    gather_rest(z, y, kv, gsem, GATHER[:NPIECE // 4])
    prepare(0)
    gather_rest(z, y, kv, gsem, GATHER[NPIECE // 4:NPIECE // 2])
    prepare(1)
    gather_rest(z, y, kv, gsem, GATHER[NPIECE // 2:])

    def tile(c, t):
        size = NY * BLOCK
        return pl.ds(pl.multiple_of(c * CK + t * size, size), size)

    def chunk(c):
        return pl.ds(pl.multiple_of(c * CK, CK), CK)

    def combine(src, dst, start, stop):
        def one(i):
            ks = pl.ds(pl.multiple_of(jnp.minimum(i + 1, LEVELS - 1) * BLOCK, BLOCK), BLOCK)
            m0 = mask_ref[2 * pos, 2 * i + 1]
            m1 = mask_ref[2 * pos + 1, 2 * i + 1]
            a0 = jnp.where(i < pos, src[0, ks, :], 0.0)
            a1 = jnp.where(i < pos, src[1, ks, :], 0.0)
            for m in range(2):
                both = jnp.where(m0 == m, a0, 0.0) + jnp.where(m1 == m, a1, 0.0)
                dst[i, m * BLOCK:(m + 1) * BLOCK, :] = both.astype(bf16)

        def four(i, _):
            for t in range(4):
                one(4 * i + t)
            return 0

        lax.fori_loop(jnp.maximum(start, 0), stop, four, 0)
        def own_level():
            for b in range(2):
                dst[pos, b * BLOCK:(b + 1) * BLOCK, :] = src[b, 0:BLOCK, :].astype(bf16)

        pl.when(stop == z + 1)(own_level)

    q_part = jnp.zeros((1, DH), f32)
    ml[3:4, 0:DH] = jnp.zeros((1, DH), f32)
    for b in range(2):
        own = 2 * pos + b

        def gather_slot(s):
            first = s == 0
            lev = jnp.where(first, pos, jnp.minimum(s - 1, pos))
            m = jnp.where(first, b, mask_ref[own, 2 * lev + 1])
            cnt = jnp.where(m == 1, count_ref[2 * lev + 1], count_ref[2 * lev])
            cnt = jnp.where(s < nl, cnt, 0)
            ks = pl.ds(pl.multiple_of(s * BLOCK, BLOCK), BLOCK)
            kx[ks, 0:128] = jnp.where(m == 1, ka[lev, 128:256], ka[lev, 0:128])
            vx[ks, 0:128] = jnp.where(m == 1, va[lev, 128:256], va[lev, 0:128])
            bias = jnp.where(sub < cnt, 0.0, NEG)
            kx[ks, 128:256] = jnp.where(lane == 0, bias, 0.0).astype(bf16)
            if b == 0:
                vx[ks, 128:256] = jnp.where(lane < 3, -1.0, 0.0).astype(bf16)

        def gather(i, _):
            for t in range(4):
                gather_slot(4 * i + t)
            return 0

        lax.fori_loop(0, nch * (LC // 4), gather, 0)
        ml[0:1, :] = jnp.full((1, R), NEG, f32)
        ml[1:2, :] = jnp.zeros((1, R), f32)

        def pass1(c, first):
            ks = chunk(c)
            kc = kx[ks, :]
            for r in range(NRT):
                rs = slice(r * RT, (r + 1) * RT)
                s = dot(kc, qT[b, :, rs])
                if first:
                    s = jnp.concatenate([s[0:BLOCK] + causal, s[BLOCK:]], axis=0)
                s_scr[ks, rs] = s
                old = ml[0:1, rs]
                new = jnp.maximum(old, jnp.max(s, axis=0, keepdims=True))
                e = jnp.exp2((s - new) * C2)
                ml[1:2, rs] = ml[1:2, rs] * jnp.exp2((old - new) * C2) + jnp.sum(e, axis=0, keepdims=True)
                ml[0:1, rs] = new

        pass1(0, True)

        def later(c, _):
            pass1(c, False)
            return 0

        lax.fori_loop(1, nch, later, 0)
        ml[2:3, :] = ml[0:1, :] * C2 + jnp.log2(ml[1:2, :])
        ot[...] = jnp.zeros_like(ot)
        dqt[...] = jnp.zeros_like(dqt)

        def forward(c, _):
            for t in range(LC // NY):
                ks = tile(c, t)
                p = jnp.exp2(s_scr[ks, :] * C2 - ml[2:3, :])
                s_scr[ks, :] = p
                low = p.astype(bf16)
                ot[...] += dot_lhs_t(vx[ks, 0:128], low)
                dv[b, ks, :] = dot(low, grows[b])
            return 0

        lax.fori_loop(0, nch, forward, 0)
        if b == 1:
            combine(dv, pv, 0, z + 1)
            scatter_leaves(z, y, 1, parts, land, ssem)
        olow = ot[...].astype(bf16)
        delta = jnp.sum(olow.astype(f32) * gT[b, 0:128, :].astype(f32), axis=0, keepdims=True)
        d0 = delta.astype(bf16)
        r1 = delta - d0.astype(f32)
        d1 = r1.astype(bf16)
        d2 = (r1 - d1.astype(f32)).astype(bf16)
        pieces = jnp.where(extra == 0, d0.astype(f32), jnp.where(extra == 1, d1.astype(f32), jnp.where(extra == 2, d2.astype(f32), 0.0)))
        gT[b, 128:256, :] = pieces.astype(bf16)
        rows = pl.ds(b * BLOCK, BLOCK)
        for i in range(HEADS):
            hs = slice(i * 128, (i + 1) * 128)
            o_scr[rows, hs] = olow[:, hs].T

        def backward(c, _):
            for t in range(LC // NY):
                ks = tile(c, t)
                kc = kx[ks, 0:128]
                dp = dot(vx[ks, :], gT[b])
                ds = (s_scr[ks, :] * dp).astype(bf16)
                dqt[...] += dot_lhs_t(kc, ds)
                acc = dot(ds, qrows[b]) * SCALE
                dk[b, ks, :] = acc
                ml[3:4, 0:DH] += jnp.sum(acc * kc.astype(f32), axis=0, keepdims=True)
            return 0

        if b == 0:
            lax.fori_loop(0, nch, backward, 0)
        else:
            early = (nch - 1) * (LC // NY - 1)
            lax.fori_loop(0, nch - 1, backward, 0)
            combine(dk, pk, 0, early)
            scatter_leaves(z, y, 0, parts, land, ssem, lambda lev: lev < NY * early)
            lax.fori_loop(nch - 1, nch, backward, 0)
            combine(dk, pk, early, z + 1)
            scatter_leaves(z, y, 0, parts, land, ssem, lambda lev: lev >= NY * early)
        for i in range(HEADS):
            hs = slice(i * 128, (i + 1) * 128)
            gqn = dqt[:, hs].T * SCALE
            hat, inv = normed(q_ref[rows, hs])
            gq_scr[rows, hs] = norm_backward(gqn, hat, inv, gain).astype(bf16)
            q_part = q_part + jnp.sum(gqn * hat, axis=0, keepdims=True)
    done = [pltpu.make_async_copy(o_scr, out_ref, lsem.at[0]), pltpu.make_async_copy(gq_scr, gq_ref, lsem.at[1])]
    for cp in done:
        cp.start()
    gains = jnp.concatenate([q_part, ml[3:4, 0:DH] / kg_ref[...], jnp.zeros((6, DH), f32)], axis=0)
    c1 = spread(arh, h, asem, 0, nh, lambda j: {"heads": lax.rem(h + j, nh)}, gains)
    third = len(SCATTER) // 3
    for x in SCATTER[:third]:
        scatter_inner(z, y, x, parts, land, ssem)
    c2 = spread(arz, z, asem, nh - 1, NZ, lambda j: {"depth": level(z, y, j, 0)}, collect(arh, nh, c1))
    for x in SCATTER[third:2 * third]:
        scatter_inner(z, y, x, parts, land, ssem)
    c3 = spread(ary, y, asem, nh + NZ - 2, NY, lambda j: {"depth": level(z, y, 0, j)}, collect(arz, NZ, c2))
    gather_drain(z, y, kv, gsem)
    for x in SCATTER[2 * third:]:
        scatter_inner(z, y, x, parts, land, ssem)
    gv_ref[...] = scatter_own(z, y, 1, parts, land, ssem).astype(bf16)
    k_hat, k_inv = normed(k_ref[...])
    gk_ref[...] = norm_backward(scatter_own(z, y, 0, parts, land, ssem), k_hat, k_inv, kg_ref[...]).astype(bf16)
    total = collect(ary, NY, c3)
    qgain_ref[...] = total[0:1]
    kgain_ref[...] = total[1:2]
    for cp in c1 + c2 + c3:
        cp.wait_send()
    scatter_drain(z, y, parts, land, ssem)
    for cp in done:
        cp.wait()


def fused(mask, count, q, g, k, v, qg, kg, nh, LC=16, RT=256):
    vmem = pl.BlockSpec(memory_space=pltpu.VMEM)
    smem = pl.BlockSpec(memory_space=pltpu.SMEM)
    hbm = pl.BlockSpec(memory_space=pl.ANY)
    sd = jax.ShapeDtypeStruct
    na = nh + NZ + NY - 3
    rows = k.shape[0]
    V = pltpu.VMEM
    dma = pltpu.SemaphoreType.DMA
    return pl.pallas_call(
        functools.partial(fused_kernel, nh, LC, RT),
        out_shape=(sd(q.shape, bf16), sd(q.shape, bf16), sd(k.shape, bf16), sd(k.shape, bf16), sd((1, DH), f32), sd((1, DH), f32)),
        in_specs=[smem, smem] + [vmem] * 6,
        out_specs=(hbm, hbm, vmem, vmem, vmem, vmem),
        scratch_shapes=[
            V((LEVELS, rows, DH), bf16), V((LEVELS, rows, DH), bf16), V((KT, 256), bf16), V((KT, 256), bf16), V((KT, R), f32),
            V((2, 256, R), bf16), V((2, 256, R), bf16), V((2, R, DH), bf16), V((2, R, DH), bf16),
            V((DH, R), f32), V((DH, R), f32), V((2, KT, DH), f32), V((2, KT, DH), f32), V((8, R), f32),
            V((LEVELS, rows, DH), bf16), V((LEVELS, rows, DH), bf16), V((NPIECE, rows // HALVES, DH), bf16),
            V(q.shape, bf16), V(q.shape, bf16),
            V((nh, 8, DH), f32), V((NZ, 8, DH), f32), V((NY, 8, DH), f32),
        ] + [dma((NPIECE,))] * 4 + [dma((na,))] * 2 + [dma((2,))],
        compiler_params=pltpu.CompilerParams(collective_id=0, has_side_effects=True, vmem_limit_bytes=60 * 2**20),
        name="tree_attention",
    )(mask, count, q, g, k, v, qg, kg)


def hand_on_kernel(*refs):
    n = len(refs) // 2
    for i in range(n):
        refs[n + i][...] = refs[i][...]


def hand_on(arrays):
    vmem = pl.BlockSpec(memory_space=pltpu.VMEM)
    n = len(arrays)
    return pl.pallas_call(
        hand_on_kernel,
        out_shape=tuple(jax.ShapeDtypeStruct(a.shape, a.dtype) for a in arrays),
        in_specs=[vmem] * n,
        out_specs=(vmem,) * n,
        name="hand_on",
    )(*arrays)


def body(q_raw, k_raw, values, q_gain, k_gain, grad_out, block_mask, block_count):
    results = fused(
        block_mask, block_count, q_raw, grad_out, k_raw, values,
        q_gain.reshape(1, DH), k_gain.reshape(1, DH), lax.axis_size("heads"),
    )
    out, gq, gk, gv, q_part, k_part = hand_on(results)
    return out, gq, gk, gv, q_part.reshape(DH), k_part.reshape(DH)


def solution(mesh):
    rows = P("depth", "heads")
    return jax.shard_map(
        body,
        mesh=mesh,
        in_specs=(rows, rows, rows, P(), P(), rows, P(), P()),
        out_specs=(rows, rows, rows, rows, P(), P()),
        check_vma=False,
    )
```
